32 devices in a mesh: layer: 2 (over x), row: 4 (over y, core), col: 4 (over z).
Axes of the slice: x: 2, y: 2, z: 4, core: 2. Of those that a mesh axis runs over, the one named last changes fastest.
Arguments:
- leaf_rhs: bfloat16 [2, 4, 4, 1, 256, 1024], P('layer', 'row', 'col'), may hold values from -6 to 6
- leaf_inv: bfloat16 [2, 4, 4, 1, 256, 256], P('layer', 'row', 'col'), may hold values from -0.6 to 1.3, as said below
- leaf_blocks: bfloat16 [2, 4, 4, 16, 256, 256], P('layer', 'row', 'col'), may hold values from -0.1875 to 0.1875
- block_col: int32 [2, 4, 4, 16], P('layer', 'row', 'col'), may hold values from 0 to 3, as said below
- block_row: int32 [2, 4, 4, 16], P('layer', 'row', 'col'), may hold values from 0 to 3, as said below
- block_count: int32 [2, 4, 4], P('layer', 'row', 'col'), may hold values from 2 to 16, as said below
- mid_rhs: bfloat16 [2, 4, 4, 256, 1024], P('layer', 'row', 'col'), may hold values from -6 to 6
- mid_inv: bfloat16 [2, 4, 4, 256, 256], P('layer', 'row', 'col'), may hold values from -0.6 to 1.3, as said below
- anc_blocks: bfloat16 [2, 4, 4, 5, 256, 256], P('layer', 'row', 'col'), may hold values from -0.0625 to 0.0625
- anc_rhs: bfloat16 [5, 256, 1024], replicated, may hold values from -6 to 6
- anc_inv: bfloat16 [5, 256, 256], replicated, may hold values from -0.6 to 1.3, as said below
- anc_lower: bfloat16 [10, 256, 256], replicated, may hold values from -0.25 to 0.25
Outputs:
- leaf_sol: bfloat16 [2, 4, 4, 1, 256, 1024], P('layer', 'row', 'col')
- mid_sol: bfloat16 [2, 4, 4, 256, 1024], P('layer', 'row', 'col')
- anc_sol: bfloat16 [5, 256, 1024], replicated
The draws below stay inside these ranges and needn't reach their ends.
Inputs may be any that keep to these rules, and one draw needn't show every extreme that they name: Entry n of a device's list names the leaf column, counted over the leaves of the device's grid column with grid rows in order, that block n multiplies; the pairs of block_col and block_row of one device are distinct. `block_row`: entry n names the mid supernode of the device's grid row, by grid column, to whose rows block n adds. The stored blocks of a device are its first block_count entries; later entries and blocks are not used. `leaf_inv`: zero above the diagonal. `mid_inv`: zero above the diagonal. `anc_inv`: zero above the diagonal.
All inputs are finite; a program needn't handle non-finite values.
Results may differ from the reference program's by a relative error of at most 0.013.
Values may be sent and summed in bfloat16 or wider, within the bound.
A program may use at most 64 MiB of HBM per device.

```python
import math
import jax
import jax.numpy as jnp
from jax import lax

S = 256
R = 1024
LEAVES = 1
BLOCKS = 16
ANCESTORS = 5
SUBTREES = 2
GRID_ROWS = 4
GRID_COLS = 4


def lower_factor(key, lead):
    key_off, key_diag = jax.random.split(key)
    strict = jax.random.normal(key_off, lead + (S, S), jnp.float32) * (0.8 / math.sqrt(S))
    strict = jnp.clip(jnp.tril(strict, -1), -0.6, 0.6)
    diagonal = jax.random.uniform(key_diag, lead + (S,), jnp.float32, 0.7, 1.3)
    identity = jnp.eye(S, dtype=jnp.float32)
    return (strict + identity * diagonal[..., None]).astype(jnp.bfloat16)


def draw_leaf_inv(key, part):
    return lower_factor(jax.random.fold_in(key, 101), (SUBTREES, GRID_ROWS, GRID_COLS, LEAVES))


def draw_mid_inv(key, part):
    return lower_factor(jax.random.fold_in(key, 102), (SUBTREES, GRID_ROWS, GRID_COLS))


def draw_anc_inv(key, part):
    return lower_factor(jax.random.fold_in(key, 103), (ANCESTORS,))


def block_pattern(key):
    devices = SUBTREES * GRID_ROWS * GRID_COLS
    pairs = GRID_ROWS * LEAVES * GRID_COLS
    device_keys = jax.random.split(jax.random.fold_in(key, 211), devices)
    chosen = jax.vmap(lambda device_key: jax.random.permutation(device_key, pairs))(device_keys)
    return chosen[:, :BLOCKS].reshape(SUBTREES, GRID_ROWS, GRID_COLS, BLOCKS).astype(jnp.int32)


def draw_block_col(key, part):
    return (block_pattern(key) // GRID_COLS).astype(jnp.int32)


def draw_block_row(key, part):
    return (block_pattern(key) % GRID_COLS).astype(jnp.int32)


def draw_block_count(key, part):
    devices = SUBTREES * GRID_ROWS * GRID_COLS
    key_counts, key_busy = jax.random.split(jax.random.fold_in(key, 307))
    counts = jax.random.randint(key_counts, (devices,), 2, BLOCKS // 2 + 1, dtype=jnp.int32)
    busiest = jax.random.randint(key_busy, (), 0, devices, dtype=jnp.int32)
    counts = jnp.where(jnp.arange(devices, dtype=jnp.int32) == busiest, BLOCKS, counts)
    return counts.reshape(SUBTREES, GRID_ROWS, GRID_COLS).astype(jnp.int32)


def level_of(rng, shape, pieces, smallest, largest):
    factor_of, own = 1.0, jax.random.fold_in(rng, 6)
    for position, parts in pieces:
        steps = jnp.exp(jax.random.uniform(jax.random.fold_in(own, position), (parts,), jnp.float32, smallest / len(pieces), largest / len(pieces)))
        factor_of = factor_of * jnp.repeat(steps, shape[position] // parts).reshape([-1 if axis == position else 1 for axis in range(len(shape))])
    return factor_of


def scatter_about(own_key, extent, width, most, cuts=(), held_as=jnp.bfloat16):
    result = jax.random.normal(own_key, extent, jnp.float32) * width
    if len(cuts) > 0:
        result = level_of(own_key, extent, cuts, -0.22, 0.18) * result
    return jnp.clip(result, min=-most, max=most).astype(held_as)


def setup_inputs(seed: int = 0) -> dict:
    arg_keys = jax.random.split(jax.random.key(seed), 13)
    leaf_rhs = scatter_about(arg_keys[0], (SUBTREES, GRID_ROWS, GRID_COLS, LEAVES, S, R), 1.0, 6.0, ((0, 2), (1, 4), (2, 4)))
    leaf_inv = draw_leaf_inv(jax.random.fold_in(arg_keys[12], 71), 0)
    leaf_blocks = scatter_about(arg_keys[2], (SUBTREES, GRID_ROWS, GRID_COLS, BLOCKS, S, S), (4 * S) ** -0.5, 0.1875, ((0, 2), (1, 4), (2, 4)))
    block_col = draw_block_col(jax.random.fold_in(arg_keys[12], 71), 0)
    block_row = draw_block_row(jax.random.fold_in(arg_keys[12], 71), 0)
    block_count = draw_block_count(jax.random.fold_in(arg_keys[12], 71), 0)
    mid_rhs = scatter_about(arg_keys[6], (SUBTREES, GRID_ROWS, GRID_COLS, S, R), 1.0, 6.0, ((0, 2), (1, 4), (2, 4)))
    mid_inv = draw_mid_inv(jax.random.fold_in(arg_keys[12], 71), 0)
    anc_blocks = scatter_about(arg_keys[8], (SUBTREES, GRID_ROWS, GRID_COLS, ANCESTORS, S, S), (S * SUBTREES * GRID_ROWS * GRID_COLS) ** -0.5, 0.0625, ((0, 2), (1, 4), (2, 4)))
    anc_rhs = scatter_about(arg_keys[9], (ANCESTORS, S, R), 1.0, 6.0)
    anc_inv = draw_anc_inv(jax.random.fold_in(arg_keys[12], 71), 0)
    anc_lower = scatter_about(arg_keys[11], (ANCESTORS * (ANCESTORS - 1) // 2, S, S), (2 * S) ** -0.5, 0.25)
    return dict(leaf_rhs=leaf_rhs, leaf_inv=leaf_inv, leaf_blocks=leaf_blocks, block_col=block_col, block_row=block_row, block_count=block_count, mid_rhs=mid_rhs, mid_inv=mid_inv, anc_blocks=anc_blocks, anc_rhs=anc_rhs, anc_inv=anc_inv, anc_lower=anc_lower)


def lower_times(factor, values):
    return jnp.einsum('...sj,...jt->...st', factor.astype(jnp.float32), values.astype(jnp.float32))


def layer_partial(inputs):
    blocks, columns, targets, counts, solutions = inputs
    grid_rows = blocks.shape[0]
    grid_cols = blocks.shape[1]
    max_blocks = blocks.shape[2]
    by_column = jnp.transpose(solutions, (1, 0, 2, 3, 4))
    by_column = by_column.reshape((grid_cols, grid_rows * solutions.shape[2]) + solutions.shape[3:])
    slot_ids = jnp.arange(max_blocks, dtype=jnp.int32)
    mid_ids = jnp.arange(grid_cols, dtype=jnp.int32)

    def row_partial(row_inputs):
        def one_column(running, scan_items):
            factor_blocks, column_ids, target_ids, live_count, column_sols = scan_items
            chosen = column_sols[column_ids].astype(jnp.float32)
            products = jnp.einsum('nsj,njt->nst', factor_blocks.astype(jnp.float32), chosen)
            live_mask = (slot_ids < live_count).astype(jnp.float32)
            placing = (target_ids[:, None] == mid_ids[None, :]).astype(jnp.float32) * live_mask[:, None]
            return running + jnp.einsum('nm,nst->mst', placing, products), None

        initial = jnp.zeros((grid_cols,) + solutions.shape[3:], jnp.float32)
        running, unused = lax.scan(one_column, initial, row_inputs + (by_column,))
        return running

    return lax.map(row_partial, (blocks, columns, targets, counts))


def reference(leaf_rhs, leaf_inv, leaf_blocks, block_col, block_row, block_count, mid_rhs, mid_inv, anc_blocks, anc_rhs, anc_inv, anc_lower):
    leaf_sol = lower_times(leaf_inv, leaf_rhs).astype(jnp.bfloat16)
    mid_partial = lax.map(layer_partial, (leaf_blocks, block_col, block_row, block_count, leaf_sol))
    mid_residue = (mid_rhs.astype(jnp.float32) - mid_partial).astype(jnp.bfloat16)
    mid_sol = lower_times(mid_inv, mid_residue).astype(jnp.bfloat16)
    anc_partial = jnp.einsum('lrcasj,lrcjt->ast', anc_blocks.astype(jnp.float32), mid_sol.astype(jnp.float32))
    solved = []
    for anc_index in range(ANCESTORS):
        running = anc_rhs[anc_index].astype(jnp.float32) - anc_partial[anc_index]
        for earlier in range(anc_index):
            packed = anc_index * (anc_index - 1) // 2 + earlier
            running = running - jnp.dot(anc_lower[packed], solved[earlier], preferred_element_type=jnp.float32)
        residue = running.astype(jnp.bfloat16)
        solved.append(jnp.dot(anc_inv[anc_index], residue, preferred_element_type=jnp.float32).astype(jnp.bfloat16))
    return leaf_sol, mid_sol, jnp.stack(solved)
```

```python
import functools

import jax
import jax.numpy as jnp
from jax import lax
from jax.experimental import pallas as pl
from jax.experimental.pallas import tpu as pltpu
from jax.sharding import PartitionSpec as P

MESH = pl.DeviceIdType.MESH
LAG = 2


def solve_ancestors(partial_rows, rhs_rows, anc_inv, anc_lower):
    solved = []
    for anc_index in range(anc_inv.shape[0]):
        running = rhs_rows[anc_index].astype(jnp.float32) - partial_rows[anc_index]
        if anc_index > 0:
            offset = anc_index * (anc_index - 1) // 2
            earlier = anc_lower[offset : offset + anc_index]
            running = running - jnp.einsum(
                "bsj,bjt->st", earlier, jnp.stack(solved), preferred_element_type=jnp.float32
            )
        residue = running.astype(jnp.bfloat16)
        solved.append(
            jnp.dot(anc_inv[anc_index], residue, preferred_element_type=jnp.float32).astype(
                jnp.bfloat16
            )
        )
    return jnp.stack(solved)


def add_slots(received):
    return jnp.sum(received, axis=0)


def body(
    leaf_rhs,
    leaf_inv,
    leaf_blocks,
    block_col,
    block_row,
    block_count,
    mid_rhs,
    mid_inv,
    anc_blocks,
    anc_rhs,
    anc_inv,
    anc_lower,
):
    leaf_sol = jnp.einsum(
        "ksj,kjt->kst", leaf_inv[0, 0, 0], leaf_rhs[0, 0, 0], preferred_element_type=jnp.float32
    ).astype(jnp.bfloat16)
    factor_blocks = leaf_blocks[0, 0, 0]
    columns = block_col[0, 0, 0]
    targets = block_row[0, 0, 0]
    live_count = block_count[0, 0, 0]
    grid_cols = lax.axis_size("col")
    empty_term = jnp.zeros((grid_cols,) + leaf_sol.shape[1:], jnp.float32)
    piece = lax.all_gather(leaf_sol, "row", axis=0, tiled=True)
    piece_rows = piece.shape[0]

    def one_block(slot_index, current_sum):
        column = columns[slot_index]
        inside = (column >= 0) & (column < piece_rows)

        def add_one(partial_sum):
            chosen = lax.dynamic_index_in_dim(
                piece, jnp.clip(column, 0, piece_rows - 1), 0, keepdims=False
            )
            product = jnp.dot(factor_blocks[slot_index], chosen, preferred_element_type=jnp.float32)
            row_now = lax.dynamic_index_in_dim(partial_sum, targets[slot_index], 0, keepdims=False)
            return lax.dynamic_update_index_in_dim(
                partial_sum, row_now + product, targets[slot_index], 0
            )

        return lax.cond(inside, add_one, lambda unchanged: unchanged, current_sum)

    mid_terms = lax.fori_loop(0, live_count, one_block, empty_term)
    mid_own = add_slots(lax.all_to_all(mid_terms, "col", split_axis=0, concat_axis=0, tiled=True))
    residue = (mid_rhs[0, 0, 0].astype(jnp.float32) - mid_own).astype(jnp.bfloat16)
    mid_sol = jnp.dot(mid_inv[0, 0, 0], residue, preferred_element_type=jnp.float32).astype(
        jnp.bfloat16
    )
    anc_term = jnp.einsum(
        "asj,jt->ast", anc_blocks[0, 0, 0], mid_sol, preferred_element_type=jnp.float32
    )
    anc_part = lax.psum(anc_term, ("layer", "row", "col"))
    anc_sol = solve_ancestors(anc_part, anc_rhs, anc_inv, anc_lower)
    return (leaf_sol[None, None, None], mid_sol[None, None, None], anc_sol)


def fused_kernel(
    layers,
    rows,
    cols,
    block_col,
    block_row,
    block_count,
    leaf_rhs_h,
    leaf_inv_h,
    blocks_h,
    mid_rhs_h,
    mid_inv_h,
    anc_blocks_h,
    anc_rhs_h,
    anc_inv_h,
    anc_lower_h,
    leaf_out,
    mid_out,
    anc_out,
    leaf_rhs,
    leaf_inv,
    blocks,
    mid_rhs,
    mid_inv,
    anc_rhs,
    anc_inv,
    anc_lower,
    xs,
    dense,
    from_left,
    from_right,
    outgoing,
    acc,
    mid_own,
    mids,
    ancb,
    part_out,
    part_outer,
    part_inner,
    total,
    sol,
    load_sem,
    store_sem,
    a_send,
    a_recv,
    b_send,
    b_recv,
    m_send,
    m_recv,
    g_send,
    g_recv,
    c_send,
    c_recv,
    s_send,
    s_recv,
):
    layer, row, col = (lax.axis_index(name) for name in ("layer", "row", "col"))
    plane = layers * rows
    size, width = mid_own.shape[1:]
    ancestors = sol.shape[0]
    max_blocks = blocks.shape[0]
    half = cols // 2
    sib_row = (row // 2) * 2 + 1 - row % 2
    far_row = (row + rows // 2) % rows
    far_sib_row = (far_row // 2) * 2 + 1 - far_row % 2
    other = (layer + 1) % layers
    sib, across, far = (layer, sib_row, col), (other, row, col), (layer, far_row, col)

    def slot(of_layer, of_row):
        return of_layer * rows + of_row

    me = slot(layer, row)

    def remote(src, dst, send_sem, recv_sem, device):
        return pltpu.make_async_remote_copy(
            src_ref=src,
            dst_ref=dst,
            send_sem=send_sem,
            recv_sem=recv_sem,
            device_id=device,
            device_id_type=MESH,
        )

    def lanes(index):
        return pl.ds(pl.multiple_of(index * width, width), width)

    loads = [
        pltpu.make_async_copy(src, dst, load_sem.at[i])
        for i, (src, dst) in enumerate(
            [
                (leaf_inv_h, leaf_inv),
                (leaf_rhs_h, leaf_rhs),
                (anc_blocks_h, ancb.at[me]),
                (blocks_h, blocks),
                (mid_rhs_h, mid_rhs),
                (mid_inv_h, mid_inv),
                (anc_rhs_h.at[:, :, lanes(me)], anc_rhs),
                (anc_inv_h, anc_inv),
                (anc_lower_h, anc_lower),
            ]
        )
    ]
    for load in loads:
        load.start()

    barrier = pltpu.get_barrier_semaphore()
    for step in range(1, plane):
        peer = (me + step) % plane
        pl.semaphore_signal(
            barrier, inc=1, device_id=(peer // rows, peer % rows, col), device_id_type=MESH
        )

    @pl.when(col > 0)
    def _():
        pl.semaphore_signal(barrier, inc=1, device_id=(layer, row, col - 1), device_id_type=MESH)

    @pl.when(col < cols - 1)
    def _():
        pl.semaphore_signal(barrier, inc=1, device_id=(layer, row, col + 1), device_id_type=MESH)

    loads[0].wait()
    loads[1].wait()
    ends = (col == 0).astype(jnp.int32) + (col == cols - 1).astype(jnp.int32)
    pl.semaphore_wait(barrier, plane + 1 - ends)

    def leaf_chunk(j, kind):
        at_row = (row, row, far_row)[kind]
        to = (sib, far, sib)[kind]
        ref = xs.at[j, at_row]
        return remote(ref, ref, a_send.at[kind, j], a_recv.at[kind, j], to)

    def leaf_arrival(j, kind):
        at_row = (sib_row, far_row, far_sib_row)[kind]
        ref = xs.at[j, at_row]
        return remote(ref, ref, a_send.at[kind, j], a_recv.at[kind, j], sib)

    def leaf_store(j):
        return pltpu.make_async_copy(
            xs.at[j, row], leaf_out.at[:, lanes(j)], store_sem.at[0, j]
        )

    def leaf_step(j, carry):
        xs[j, row] = jnp.dot(
            leaf_inv[...], leaf_rhs[:, lanes(j)], preferred_element_type=jnp.float32
        ).astype(xs.dtype)
        leaf_chunk(j, 1).start()
        leaf_chunk(j, 0).start()
        leaf_store(j).start()
        return carry

    lax.fori_loop(0, plane, leaf_step, 0)

    def block_copy(kind):
        which = (me, me, me, slot(other, row), slot(layer, far_row), slot(layer, far_row))
        which = (which + (slot(other, far_row),))[kind]
        to = (sib, across, far, sib, sib, across, sib)[kind]
        ref = ancb.at[which]
        return remote(ref, ref, g_send.at[kind], g_recv.at[kind], to)

    def block_arrival(kind):
        which = (
            slot(layer, sib_row),
            slot(other, row),
            slot(layer, far_row),
            slot(other, sib_row),
            slot(layer, far_sib_row),
            slot(other, far_row),
            slot(other, far_sib_row),
        )[kind]
        ref = ancb.at[which]
        return remote(ref, ref, g_send.at[kind], g_recv.at[kind], sib)

    loads[2].wait()
    block_copy(1).start()
    block_copy(0).start()

    loads[3].wait()

    def place_target(m, carry):
        for i in range(rows):
            found = jnp.int32(max_blocks)
            for n in range(max_blocks):
                hit = (block_col[n] == i) & (block_row[n] == m) & (n < block_count[0])
                found = jnp.where(hit, n, found)
            there = found < max_blocks
            block = blocks[jnp.minimum(found, max_blocks - 1)]
            keep = jnp.full(block.shape, there.astype(jnp.int32)) > 0
            dense[m, :, i * size : (i + 1) * size] = jnp.where(
                keep, block.astype(jnp.float32), 0.0
            ).astype(dense.dtype)
        return carry

    lax.fori_loop(0, cols, place_target, 0)

    def gathered(j):
        return xs[j].reshape(rows * size, width)

    def sum_copy(j, m, buffer, to):
        return remote(outgoing.at[j, m], buffer.at[j, m], b_send.at[j, m], b_recv_of(buffer, j, m), to)

    def b_recv_of(buffer, j, m):
        return b_recv.at[0 if buffer is from_left else 1, j, m]

    def sums_on(j, m, buffer, has_more, to):
        outgoing_sum = jnp.dot(dense[m], gathered(j), preferred_element_type=jnp.float32)

        @pl.when(has_more)
        def _():
            sum_copy(j, m, buffer, to).wait_recv()
            outgoing[j, m] = (outgoing_sum + buffer[j, m].astype(jnp.float32)).astype(
                outgoing.dtype
            )

        @pl.when(jnp.logical_not(has_more))
        def _():
            outgoing[j, m] = outgoing_sum.astype(outgoing.dtype)

        sum_copy(j, m, buffer, to).start()

    def mid_copy(j):
        return remote(
            mid_own.at[j], mids.at[me], m_send.at[j], m_recv.at[me], (j // rows, j % rows, col)
        )

    def mid_store(j):
        return pltpu.make_async_copy(mid_own.at[j], mid_out.at[:, lanes(j)], store_sem.at[1, j])

    def forward_leaf(j):
        leaf_arrival(j, 1).wait_recv()
        leaf_chunk(j, 2).start()

    loads[4].wait()
    loads[5].wait()
    forward_leaf(0)

    def sum_step(j, carry):
        @pl.when(j < plane)
        def _():
            @pl.when(j < plane - 1)
            def _():
                forward_leaf(j + 1)

            leaf_arrival(j, 0).wait_recv()
            leaf_arrival(j, 2).wait_recv()
            for distance in range(cols - 1, 0, -1):

                @pl.when(col + distance < cols)
                def _():
                    sums_on(j, col + distance, from_left, col > 0, (layer, row, col + 1))

                @pl.when(col - distance >= 0)
                def _():
                    sums_on(j, col - distance, from_right, col < cols - 1, (layer, row, col - 1))

        @pl.when(j == 3)
        def _():
            block_copy(2).start()

        @pl.when(j == 4)
        def _():
            block_arrival(1).wait_recv()
            block_copy(3).start()

        @pl.when(j == plane - 1)
        def _():
            block_arrival(2).wait_recv()
            block_copy(5).start()
            block_copy(4).start()

        @pl.when(j >= LAG)
        def _():
            done = j - LAG
            acc[...] = mid_rhs[:, lanes(done)].astype(jnp.float32) - jnp.dot(
                dense[col], gathered(done), preferred_element_type=jnp.float32
            )

            @pl.when(col > 0)
            def _():
                sum_copy(done, col, from_left, sib).wait_recv()
                acc[...] -= from_left[done, col].astype(jnp.float32)

            @pl.when(col < cols - 1)
            def _():
                sum_copy(done, col, from_right, sib).wait_recv()
                acc[...] -= from_right[done, col].astype(jnp.float32)

            solved = jnp.dot(
                mid_inv[...], acc[...].astype(jnp.bfloat16), preferred_element_type=jnp.float32
            ).astype(jnp.bfloat16)
            mid_own[done] = solved

            @pl.when(done == me)
            def _():
                mids[me] = solved

            @pl.when(done != me)
            def _():
                mid_copy(done).start()

            mid_store(done).start()

        return carry

    lax.fori_loop(0, plane + LAG, sum_step, 0)

    block_arrival(5).wait_recv()
    block_copy(6).start()
    for kind in (0, 3, 4, 6):
        block_arrival(kind).wait_recv()
    for step in range(1, plane):
        peer = (me + step) % plane
        remote(mids.at[peer], mids.at[peer], m_send.at[0], m_recv.at[peer], sib).wait_recv()
    for load in loads[6:]:
        load.wait()

    in_left = col < half
    inward = (layer, row, jnp.where(in_left, col + 1, col - 1))
    outward = (layer, row, jnp.where(in_left, col - 1, col + 1))
    middle = (col == half - 1) | (col == half)
    has_outer = (col > 0) & (col < cols - 1)

    def up_copy(a, buffer, kind, to):
        return remote(part_out.at[a], buffer.at[a], c_send.at[0, a], c_recv.at[kind, a], to)

    def down_copy(a):
        return remote(total.at[a], part_inner.at[a], c_send.at[1, a], c_recv.at[1, a], outward)

    for a in range(ancestors):
        term = jnp.zeros((size, width), jnp.float32)
        for k in range(plane):
            term += jnp.dot(ancb[k, a], mids[k], preferred_element_type=jnp.float32)
        acc[...] = term

        @pl.when(has_outer)
        def _():
            up_copy(a, part_outer, 0, sib).wait_recv()
            acc[...] += part_outer[a].astype(jnp.float32)

        part_out[a] = acc[...].astype(part_out.dtype)

        @pl.when(middle)
        def _():
            up_copy(a, part_inner, 1, inward).start()

        @pl.when(jnp.logical_not(middle))
        def _():
            up_copy(a, part_outer, 0, inward).start()

    def sol_ref(a, which):
        return anc_out.at[a, :, lanes(which)]

    def sol_copy(a, kind):
        relay = a % 2
        which = (
            me,
            me,
            me,
            slot(other, row),
            slot(layer, far_row),
            (slot(other, row), slot(layer, far_row))[relay],
            slot(other, far_row),
        )[kind]
        to = (sib, across, far, sib, sib, (far, across)[relay], sib)[kind]
        src = sol.at[a] if kind < 3 else sol_ref(a, which)
        return remote(src, sol_ref(a, which), s_send.at[kind, a], s_recv.at[kind, a], to)

    def sol_arrival(a, kind):
        which = (
            slot(layer, sib_row),
            slot(other, row),
            slot(layer, far_row),
            slot(other, sib_row),
            slot(layer, far_sib_row),
            slot(other, far_row),
            slot(other, far_sib_row),
        )[kind]
        return remote(sol.at[a], sol_ref(a, which), s_send.at[kind, a], s_recv.at[kind, a], sib)

    def sol_store(a):
        return pltpu.make_async_copy(sol.at[a], sol_ref(a, me), store_sem.at[2, a])

    for a in range(ancestors):
        up_copy(a, part_inner, 1, sib).wait_recv()

        @pl.when(middle)
        def _():
            total[a] = (
                part_out[a].astype(jnp.float32) + part_inner[a].astype(jnp.float32)
            ).astype(total.dtype)

        @pl.when(jnp.logical_not(middle))
        def _():
            total[a] = part_inner[a]

        @pl.when(has_outer)
        def _():
            down_copy(a).start()

        running = anc_rhs[a].astype(jnp.float32) - total[a].astype(jnp.float32)
        offset = a * (a - 1) // 2
        for b in range(a):
            running -= jnp.dot(anc_lower[offset + b], sol[b], preferred_element_type=jnp.float32)
        sol[a] = jnp.dot(
            anc_inv[a], running.astype(jnp.bfloat16), preferred_element_type=jnp.float32
        ).astype(sol.dtype)
        for kind in (2, 1, 0):
            sol_copy(a, kind).start()
        sol_store(a).start()

    for a in range(ancestors):
        for kind in ((1, 2), (2, 1))[a % 2]:
            sol_arrival(a, kind).wait_recv()
            if kind == 1 + a % 2:
                sol_copy(a, 5).start()
            sol_copy(a, kind + 2).start()
    for a in range(ancestors):
        sol_arrival(a, 5).wait_recv()
        sol_copy(a, 6).start()

    def drain(j, carry):
        for kind in range(3):
            leaf_chunk(j, kind).wait_send()
        leaf_store(j).wait()
        mid_store(j).wait()

        @pl.when(j != me)
        def _():
            mid_copy(j).wait_send()

        def drain_sums(m, inner):
            @pl.when(m != col)
            def _():
                sum_copy(j, m, from_left, sib).wait_send()

            return inner

        lax.fori_loop(0, cols, drain_sums, 0)
        return carry

    lax.fori_loop(0, plane, drain, 0)
    for kind in range(7):
        block_copy(kind).wait_send()
    for a in range(ancestors):
        up_copy(a, part_inner, 1, sib).wait_send()

        @pl.when(has_outer)
        def _():
            down_copy(a).wait_send()

        for kind in range(7):
            sol_copy(a, kind).wait_send()
        sol_store(a).wait()
        for kind in (0, 3, 4, 6):
            sol_arrival(a, kind).wait_recv()


def fused_body(
    layers,
    rows,
    cols,
    leaf_rhs,
    leaf_inv,
    leaf_blocks,
    block_col,
    block_row,
    block_count,
    mid_rhs,
    mid_inv,
    anc_blocks,
    anc_rhs,
    anc_inv,
    anc_lower,
):
    plane = layers * rows
    size, rhs_count = mid_rhs.shape[-2:]
    ancestors = anc_inv.shape[0]
    max_blocks = leaf_blocks.shape[3]
    width = rhs_count // plane
    kept = mid_rhs.dtype
    smem = pl.BlockSpec(memory_space=pltpu.SMEM)
    hbm = pl.BlockSpec(memory_space=pl.ANY)
    dma = pltpu.SemaphoreType.DMA
    vmem = pltpu.VMEM
    leaf_sol, mid_sol, anc_sol = pl.pallas_call(
        functools.partial(fused_kernel, layers, rows, cols),
        out_shape=[
            jax.ShapeDtypeStruct((size, rhs_count), kept),
            jax.ShapeDtypeStruct((size, rhs_count), kept),
            jax.ShapeDtypeStruct((ancestors, size, rhs_count), kept),
        ],
        in_specs=[smem] * 3 + [hbm] * 9,
        out_specs=[hbm] * 3,
        scratch_shapes=[
            vmem((size, rhs_count), kept),
            vmem((size, size), kept),
            vmem((max_blocks, size, size), kept),
            vmem((size, rhs_count), kept),
            vmem((size, size), kept),
            vmem((ancestors, size, width), kept),
            vmem(anc_inv.shape, kept),
            vmem(anc_lower.shape, kept),
            vmem((plane, rows, size, width), kept),
            vmem((cols, size, rows * size), kept),
            vmem((plane, cols, size, width), kept),
            vmem((plane, cols, size, width), kept),
            vmem((plane, cols, size, width), kept),
            vmem((size, width), jnp.float32),
            vmem((plane, size, width), kept),
            vmem((plane, size, width), kept),
            vmem((plane, ancestors, size, size), kept),
            vmem((ancestors, size, width), kept),
            vmem((ancestors, size, width), kept),
            vmem((ancestors, size, width), kept),
            vmem((ancestors, size, width), kept),
            vmem((ancestors, size, width), kept),
            dma((9,)),
            dma((3, max(plane, ancestors))),
            dma((3, plane)),
            dma((3, plane)),
            dma((plane, cols)),
            dma((2, plane, cols)),
            dma((plane,)),
            dma((plane,)),
            dma((7,)),
            dma((7,)),
            dma((2, ancestors)),
            dma((2, ancestors)),
            dma((7, ancestors)),
            dma((7, ancestors)),
        ],
        compiler_params=pltpu.CompilerParams(
            collective_id=0, has_side_effects=True, vmem_limit_bytes=48 * 1024 * 1024
        ),
        name="fused_solve",
    )(
        block_col[0, 0, 0],
        block_row[0, 0, 0],
        block_count[0, 0],
        leaf_rhs[0, 0, 0, 0],
        leaf_inv[0, 0, 0, 0],
        leaf_blocks[0, 0, 0],
        mid_rhs[0, 0, 0],
        mid_inv[0, 0, 0],
        anc_blocks[0, 0, 0],
        anc_rhs,
        anc_inv,
        anc_lower,
    )
    return (leaf_sol[None, None, None, None], mid_sol[None, None, None], anc_sol)


def fits_fused(mesh, rhs_count):
    layers, rows, cols = (mesh.shape[name] for name in ("layer", "row", "col"))
    pairs = layers == 2 and rows == 4 and cols % 2 == 0
    return pairs and rhs_count % (layers * rows * 128) == 0


def solution(mesh):
    in_specs = (
        P("layer", "row", "col", None, None, None),
        P("layer", "row", "col", None, None, None),
        P("layer", "row", "col", None, None, None),
        P("layer", "row", "col", None),
        P("layer", "row", "col", None),
        P("layer", "row", "col"),
        P("layer", "row", "col", None, None),
        P("layer", "row", "col", None, None),
        P("layer", "row", "col", None, None, None),
        P(),
        P(),
        P(),
    )
    out_specs = (
        P("layer", "row", "col", None, None, None),
        P("layer", "row", "col", None, None),
        P(),
    )

    def run(leaf_rhs, *rest):
        chosen = body
        if fits_fused(mesh, leaf_rhs.shape[-1]) and leaf_rhs.shape[3] == 1:
            sizes = (mesh.shape[name] for name in ("layer", "row", "col"))
            chosen = functools.partial(fused_body, *sizes)
        return jax.shard_map(
            chosen, mesh=mesh, in_specs=in_specs, out_specs=out_specs, check_vma=False
        )(leaf_rhs, *rest)

    return run
```

```python
import functools

import jax
import jax.numpy as jnp
from jax import lax
from jax.experimental import pallas as pl
from jax.experimental.pallas import tpu as pltpu
from jax.sharding import PartitionSpec as P

MESH = pl.DeviceIdType.MESH
LAG = 4


def solve_ancestors(partial_rows, rhs_rows, anc_inv, anc_lower):
    solved = []
    for anc_index in range(anc_inv.shape[0]):
        running = rhs_rows[anc_index].astype(jnp.float32) - partial_rows[anc_index]
        if anc_index > 0:
            offset = anc_index * (anc_index - 1) // 2
            earlier = anc_lower[offset : offset + anc_index]
            running = running - jnp.einsum(
                "bsj,bjt->st", earlier, jnp.stack(solved), preferred_element_type=jnp.float32
            )
        residue = running.astype(jnp.bfloat16)
        solved.append(
            jnp.dot(anc_inv[anc_index], residue, preferred_element_type=jnp.float32).astype(
                jnp.bfloat16
            )
        )
    return jnp.stack(solved)


def add_slots(received):
    return jnp.sum(received, axis=0)


def body(
    leaf_rhs,
    leaf_inv,
    leaf_blocks,
    block_col,
    block_row,
    block_count,
    mid_rhs,
    mid_inv,
    anc_blocks,
    anc_rhs,
    anc_inv,
    anc_lower,
):
    leaf_sol = jnp.einsum(
        "ksj,kjt->kst", leaf_inv[0, 0, 0], leaf_rhs[0, 0, 0], preferred_element_type=jnp.float32
    ).astype(jnp.bfloat16)
    factor_blocks = leaf_blocks[0, 0, 0]
    columns = block_col[0, 0, 0]
    targets = block_row[0, 0, 0]
    live_count = block_count[0, 0, 0]
    grid_cols = lax.axis_size("col")
    empty_term = jnp.zeros((grid_cols,) + leaf_sol.shape[1:], jnp.float32)
    piece = lax.all_gather(leaf_sol, "row", axis=0, tiled=True)
    piece_rows = piece.shape[0]

    def one_block(slot_index, current_sum):
        column = columns[slot_index]
        inside = (column >= 0) & (column < piece_rows)

        def add_one(partial_sum):
            chosen = lax.dynamic_index_in_dim(
                piece, jnp.clip(column, 0, piece_rows - 1), 0, keepdims=False
            )
            product = jnp.dot(factor_blocks[slot_index], chosen, preferred_element_type=jnp.float32)
            row_now = lax.dynamic_index_in_dim(partial_sum, targets[slot_index], 0, keepdims=False)
            return lax.dynamic_update_index_in_dim(
                partial_sum, row_now + product, targets[slot_index], 0
            )

        return lax.cond(inside, add_one, lambda unchanged: unchanged, current_sum)

    mid_terms = lax.fori_loop(0, live_count, one_block, empty_term)
    mid_own = add_slots(lax.all_to_all(mid_terms, "col", split_axis=0, concat_axis=0, tiled=True))
    residue = (mid_rhs[0, 0, 0].astype(jnp.float32) - mid_own).astype(jnp.bfloat16)
    mid_sol = jnp.dot(mid_inv[0, 0, 0], residue, preferred_element_type=jnp.float32).astype(
        jnp.bfloat16
    )
    anc_term = jnp.einsum(
        "asj,jt->ast", anc_blocks[0, 0, 0], mid_sol, preferred_element_type=jnp.float32
    )
    anc_part = lax.psum(anc_term, ("layer", "row", "col"))
    anc_sol = solve_ancestors(anc_part, anc_rhs, anc_inv, anc_lower)
    return (leaf_sol[None, None, None], mid_sol[None, None, None], anc_sol)


def fused_kernel(
    layers,
    rows,
    cols,
    block_col_h,
    block_row_h,
    block_count_h,
    leaf_rhs_h,
    leaf_inv_h,
    blocks_h,
    mid_rhs_h,
    mid_inv_h,
    anc_blocks_h,
    anc_rhs_h,
    anc_inv_h,
    anc_lower_h,
    leaf_out,
    mid_out,
    anc_out,
    block_col,
    block_row,
    block_count,
    leaf_rhs,
    leaf_inv,
    blocks,
    mid_rhs,
    mid_inv,
    anc_rhs,
    anc_inv,
    anc_lower,
    xs,
    dense,
    from_left,
    from_right,
    outgoing,
    acc,
    mid_own,
    mids,
    ancb,
    part_out,
    part_outer,
    part_inner,
    total,
    sol,
    load_sem,
    store_sem,
    a_send,
    a_recv,
    b_send,
    b_recv,
    m_send,
    m_recv,
    g_send,
    g_recv,
    c_send,
    c_recv,
    s_send,
    s_recv,
):
    layer, row, col = (lax.axis_index(name) for name in ("layer", "row", "col"))
    plane = layers * rows
    size, width = mid_own.shape[1:]
    ancestors = sol.shape[0]
    max_blocks = blocks.shape[0]
    half = cols // 2
    sib_row = (row // 2) * 2 + 1 - row % 2
    far_row = (row + rows // 2) % rows
    far_sib_row = (far_row // 2) * 2 + 1 - far_row % 2
    other = (layer + 1) % layers
    sib, across, far = (layer, sib_row, col), (other, row, col), (layer, far_row, col)

    def slot(of_layer, of_row):
        return of_layer * rows + of_row

    me = slot(layer, row)

    def remote(src, dst, send_sem, recv_sem, device):
        return pltpu.make_async_remote_copy(
            src_ref=src,
            dst_ref=dst,
            send_sem=send_sem,
            recv_sem=recv_sem,
            device_id=device,
            device_id_type=MESH,
        )

    def lanes(index):
        return pl.ds(pl.multiple_of(index * width, width), width)

    def depth_of(which):
        return pl.ds(pl.multiple_of(which * size, size), size)

    loads = [
        pltpu.make_async_copy(src, dst, load_sem.at[i])
        for i, (src, dst) in enumerate(
            [
                (leaf_inv_h, leaf_inv),
                (leaf_rhs_h, leaf_rhs),
                (anc_blocks_h, ancb.at[:, :, depth_of(me)]),
                (blocks_h, blocks),
                (mid_rhs_h, mid_rhs),
                (mid_inv_h, mid_inv),
                (anc_rhs_h.at[:, :, lanes(me)], anc_rhs),
                (anc_inv_h, anc_inv),
                (anc_lower_h, anc_lower),
                (block_col_h, block_col),
                (block_row_h, block_row),
                (block_count_h, block_count),
            ]
        )
    ]
    for load in loads:
        load.start()

    barrier = pltpu.get_barrier_semaphore()
    for step in range(1, plane):
        peer = (me + step) % plane
        pl.semaphore_signal(
            barrier, inc=1, device_id=(peer // rows, peer % rows, col), device_id_type=MESH
        )

    @pl.when(col > 0)
    def _():
        pl.semaphore_signal(barrier, inc=1, device_id=(layer, row, col - 1), device_id_type=MESH)

    @pl.when(col < cols - 1)
    def _():
        pl.semaphore_signal(barrier, inc=1, device_id=(layer, row, col + 1), device_id_type=MESH)

    loads[0].wait()
    loads[1].wait()
    ends = (col == 0).astype(jnp.int32) + (col == cols - 1).astype(jnp.int32)
    pl.semaphore_wait(barrier, plane + 1 - ends)

    def leaf_chunk(j, kind):
        at_row = (row, row, far_row)[kind]
        to = (sib, far, sib)[kind]
        ref = xs.at[j, at_row]
        return remote(ref, ref, a_send.at[kind, j], a_recv.at[kind, j], to)

    def leaf_arrival(j, kind):
        at_row = (sib_row, far_row, far_sib_row)[kind]
        ref = xs.at[j, at_row]
        return remote(ref, ref, a_send.at[kind, j], a_recv.at[kind, j], sib)

    def leaf_store(j):
        return pltpu.make_async_copy(
            xs.at[j, row], leaf_out.at[:, lanes(j)], store_sem.at[0, j]
        )

    def leaf_step(j, carry):
        xs[j, row] = jnp.dot(
            leaf_inv[...], leaf_rhs[:, lanes(j)], preferred_element_type=jnp.float32
        ).astype(xs.dtype)
        leaf_chunk(j, 1).start()
        leaf_chunk(j, 0).start()
        leaf_store(j).start()
        return carry

    lax.fori_loop(0, plane, leaf_step, 0)

    def block_copy(kind):
        which = (me, me, me, slot(other, row), slot(layer, far_row), slot(layer, far_row))
        which = (which + (slot(other, far_row),))[kind]
        to = (sib, across, far, sib, sib, across, sib)[kind]
        ref = ancb.at[:, :, depth_of(which)]
        return remote(ref, ref, g_send.at[kind], g_recv.at[kind], to)

    def block_arrival(kind):
        which = (
            slot(layer, sib_row),
            slot(other, row),
            slot(layer, far_row),
            slot(other, sib_row),
            slot(layer, far_sib_row),
            slot(other, far_row),
            slot(other, far_sib_row),
        )[kind]
        ref = ancb.at[:, :, depth_of(which)]
        return remote(ref, ref, g_send.at[kind], g_recv.at[kind], sib)

    loads[2].wait()
    block_copy(1).start()
    block_copy(2).start()
    block_copy(0).start()

    for load in loads[9:] + loads[3:4]:
        load.wait()

    def place_target(m, carry):
        for i in range(rows):
            found = jnp.int32(max_blocks)
            for n in range(max_blocks):
                hit = (block_col[n] == i) & (block_row[n] == m) & (n < block_count[0, 0, 0])
                found = jnp.where(hit, n, found)
            there = found < max_blocks
            block = blocks[jnp.minimum(found, max_blocks - 1)]
            keep = jnp.full(block.shape, there.astype(jnp.int32)) > 0
            dense[m, :, i * size : (i + 1) * size] = jnp.where(
                keep, block.astype(jnp.float32), 0.0
            ).astype(dense.dtype)
        return carry

    lax.fori_loop(0, cols, place_target, 0)

    def gathered(j):
        return xs[j].reshape(rows * size, width)

    def sum_copy(j, m, buffer, to):
        return remote(outgoing.at[j, m], buffer.at[j, m], b_send.at[j, m], b_recv_of(buffer, j, m), to)

    def b_recv_of(buffer, j, m):
        return b_recv.at[0 if buffer is from_left else 1, j, m]

    def sums_on(j, m, buffer, has_more, to):
        outgoing_sum = jnp.dot(dense[m], gathered(j), preferred_element_type=jnp.float32)

        @pl.when(has_more)
        def _():
            sum_copy(j, m, buffer, to).wait_recv()
            outgoing[j, m] = (outgoing_sum + buffer[j, m].astype(jnp.float32)).astype(
                outgoing.dtype
            )

        @pl.when(jnp.logical_not(has_more))
        def _():
            outgoing[j, m] = outgoing_sum.astype(outgoing.dtype)

        sum_copy(j, m, buffer, to).start()

    def mid_copy(j):
        return remote(
            mid_own.at[j], mids.at[me], m_send.at[j], m_recv.at[me], (j // rows, j % rows, col)
        )

    def mid_store(j):
        return pltpu.make_async_copy(mid_own.at[j], mid_out.at[:, lanes(j)], store_sem.at[1, j])

    def forward_leaf(j):
        leaf_arrival(j, 1).wait_recv()
        leaf_chunk(j, 2).start()

    loads[4].wait()
    loads[5].wait()
    forward_leaf(0)

    def sum_step(j, carry):
        @pl.when(j < plane)
        def _():
            @pl.when(j < plane - 1)
            def _():
                forward_leaf(j + 1)

            leaf_arrival(j, 0).wait_recv()
            leaf_arrival(j, 2).wait_recv()
            for distance in range(cols - 1, 0, -1):

                @pl.when(col + distance < cols)
                def _():
                    sums_on(j, col + distance, from_left, col > 0, (layer, row, col + 1))

                @pl.when(col - distance >= 0)
                def _():
                    sums_on(j, col - distance, from_right, col < cols - 1, (layer, row, col - 1))

        @pl.when(j == 3)
        def _():
            block_arrival(1).wait_recv()
            block_copy(3).start()

        @pl.when(j == 6)
        def _():
            block_arrival(2).wait_recv()
            block_copy(5).start()
            block_copy(4).start()

        @pl.when(j >= LAG)
        def _():
            done = j - LAG
            acc[...] = mid_rhs[:, lanes(done)].astype(jnp.float32) - jnp.dot(
                dense[col], gathered(done), preferred_element_type=jnp.float32
            )

            @pl.when(col > 0)
            def _():
                sum_copy(done, col, from_left, sib).wait_recv()
                acc[...] -= from_left[done, col].astype(jnp.float32)

            @pl.when(col < cols - 1)
            def _():
                sum_copy(done, col, from_right, sib).wait_recv()
                acc[...] -= from_right[done, col].astype(jnp.float32)

            solved = jnp.dot(
                mid_inv[...], acc[...].astype(jnp.bfloat16), preferred_element_type=jnp.float32
            ).astype(jnp.bfloat16)
            mid_own[done] = solved

            @pl.when(done == me)
            def _():
                mids[me] = solved

            @pl.when(done != me)
            def _():
                mid_copy(done).start()

            mid_store(done).start()

        return carry

    lax.fori_loop(0, plane + LAG, sum_step, 0)

    block_arrival(5).wait_recv()
    block_copy(6).start()
    for kind in (0, 3, 4, 6):
        block_arrival(kind).wait_recv()
    for step in range(1, plane):
        peer = (me + step) % plane
        remote(mids.at[peer], mids.at[peer], m_send.at[0], m_recv.at[peer], sib).wait_recv()
    for load in loads[6:9]:
        load.wait()

    in_left = col < half
    inward = (layer, row, jnp.where(in_left, col + 1, col - 1))
    outward = (layer, row, jnp.where(in_left, col - 1, col + 1))
    middle = (col == half - 1) | (col == half)
    has_outer = (col > 0) & (col < cols - 1)

    def up_copy(a, buffer, kind, to):
        return remote(part_out.at[a], buffer.at[a], c_send.at[0, a], c_recv.at[kind, a], to)

    def down_copy(a):
        return remote(total.at[a], part_inner.at[a], c_send.at[1, a], c_recv.at[1, a], outward)

    for a in range(ancestors):
        acc[...] = jnp.dot(
            ancb[a], mids[...].reshape(plane * size, width), preferred_element_type=jnp.float32
        )

        @pl.when(has_outer)
        def _():
            up_copy(a, part_outer, 0, sib).wait_recv()
            acc[...] += part_outer[a].astype(jnp.float32)

        part_out[a] = acc[...].astype(part_out.dtype)

        @pl.when(middle)
        def _():
            up_copy(a, part_inner, 1, inward).start()

        @pl.when(jnp.logical_not(middle))
        def _():
            up_copy(a, part_outer, 0, inward).start()

    def sol_ref(a, which):
        return anc_out.at[a, :, lanes(which)]

    def sol_copy(a, kind):
        relay = a % 2
        which = (
            me,
            me,
            me,
            slot(other, row),
            slot(layer, far_row),
            (slot(other, row), slot(layer, far_row))[relay],
            slot(other, far_row),
        )[kind]
        to = (sib, across, far, sib, sib, (far, across)[relay], sib)[kind]
        src = sol.at[a] if kind < 3 else sol_ref(a, which)
        return remote(src, sol_ref(a, which), s_send.at[kind, a], s_recv.at[kind, a], to)

    def sol_arrival(a, kind):
        which = (
            slot(layer, sib_row),
            slot(other, row),
            slot(layer, far_row),
            slot(other, sib_row),
            slot(layer, far_sib_row),
            slot(other, far_row),
            slot(other, far_sib_row),
        )[kind]
        return remote(sol.at[a], sol_ref(a, which), s_send.at[kind, a], s_recv.at[kind, a], sib)

    def sol_store(a):
        return pltpu.make_async_copy(sol.at[a], sol_ref(a, me), store_sem.at[2, a])

    for a in range(ancestors):
        up_copy(a, part_inner, 1, sib).wait_recv()

        @pl.when(middle)
        def _():
            total[a] = (
                part_out[a].astype(jnp.float32) + part_inner[a].astype(jnp.float32)
            ).astype(total.dtype)

        @pl.when(jnp.logical_not(middle))
        def _():
            total[a] = part_inner[a]

        @pl.when(has_outer)
        def _():
            down_copy(a).start()

        running = anc_rhs[a].astype(jnp.float32) - total[a].astype(jnp.float32)
        offset = a * (a - 1) // 2
        for b in range(a):
            running -= jnp.dot(anc_lower[offset + b], sol[b], preferred_element_type=jnp.float32)
        sol[a] = jnp.dot(
            anc_inv[a], running.astype(jnp.bfloat16), preferred_element_type=jnp.float32
        ).astype(sol.dtype)
        for kind in (2, 1, 0):
            sol_copy(a, kind).start()
        sol_store(a).start()

    for a in range(ancestors):
        for kind in ((1, 2), (2, 1))[a % 2]:
            sol_arrival(a, kind).wait_recv()
            if kind == 1 + a % 2:
                sol_copy(a, 5).start()
            sol_copy(a, kind + 2).start()
    for a in range(ancestors):
        sol_arrival(a, 5).wait_recv()
        sol_copy(a, 6).start()

    def drain(j, carry):
        for kind in range(3):
            leaf_chunk(j, kind).wait_send()
        leaf_store(j).wait()
        mid_store(j).wait()

        @pl.when(j != me)
        def _():
            mid_copy(j).wait_send()

        def drain_sums(m, inner):
            @pl.when(m != col)
            def _():
                sum_copy(j, m, from_left, sib).wait_send()

            return inner

        lax.fori_loop(0, cols, drain_sums, 0)
        return carry

    lax.fori_loop(0, plane, drain, 0)
    for kind in range(7):
        block_copy(kind).wait_send()
    for a in range(ancestors):
        up_copy(a, part_inner, 1, sib).wait_send()

        @pl.when(has_outer)
        def _():
            down_copy(a).wait_send()

        for kind in range(7):
            sol_copy(a, kind).wait_send()
        sol_store(a).wait()
        for kind in (0, 3, 4, 6):
            sol_arrival(a, kind).wait_recv()


def place_results(leaf_in, mid_in, anc_in, leaf_out, mid_out, anc_out, sem):
    copies = [
        pltpu.make_async_copy(anc_in.at[a], anc_out.at[a], sem.at[a])
        for a in range(anc_in.shape[0])
    ]
    copies.append(pltpu.make_async_copy(leaf_in, leaf_out, sem.at[len(copies)]))
    copies.append(pltpu.make_async_copy(mid_in, mid_out, sem.at[len(copies)]))
    for copy in copies:
        copy.start()
    for copy in copies:
        copy.wait()


def fused_body(
    layers,
    rows,
    cols,
    leaf_rhs,
    leaf_inv,
    leaf_blocks,
    block_col,
    block_row,
    block_count,
    mid_rhs,
    mid_inv,
    anc_blocks,
    anc_rhs,
    anc_inv,
    anc_lower,
):
    plane = layers * rows
    size, rhs_count = mid_rhs.shape[-2:]
    ancestors = anc_inv.shape[0]
    max_blocks = leaf_blocks.shape[3]
    width = rhs_count // plane
    kept = mid_rhs.dtype
    anywhere = pl.BlockSpec(memory_space=pl.ANY)
    hbm = pl.BlockSpec(memory_space=pltpu.HBM)
    dma = pltpu.SemaphoreType.DMA
    vmem = pltpu.VMEM
    leaf_sol, mid_sol, anc_sol = pl.pallas_call(
        functools.partial(fused_kernel, layers, rows, cols),
        out_shape=[
            jax.ShapeDtypeStruct((size, rhs_count), kept),
            jax.ShapeDtypeStruct((size, rhs_count), kept),
            jax.ShapeDtypeStruct((ancestors, size, rhs_count), kept),
        ],
        in_specs=[hbm] * 12,
        out_specs=[anywhere] * 3,
        scratch_shapes=[
            pltpu.SMEM((max_blocks,), jnp.int32),
            pltpu.SMEM((max_blocks,), jnp.int32),
            pltpu.SMEM(block_count.shape, jnp.int32),
            vmem((size, rhs_count), kept),
            vmem((size, size), kept),
            vmem((max_blocks, size, size), kept),
            vmem((size, rhs_count), kept),
            vmem((size, size), kept),
            vmem((ancestors, size, width), kept),
            vmem(anc_inv.shape, kept),
            vmem(anc_lower.shape, kept),
            vmem((plane, rows, size, width), kept),
            vmem((cols, size, rows * size), kept),
            vmem((plane, cols, size, width), kept),
            vmem((plane, cols, size, width), kept),
            vmem((plane, cols, size, width), kept),
            vmem((size, width), jnp.float32),
            vmem((plane, size, width), kept),
            vmem((plane, size, width), kept),
            vmem((ancestors, size, plane * size), kept),
            vmem((ancestors, size, width), kept),
            vmem((ancestors, size, width), kept),
            vmem((ancestors, size, width), kept),
            vmem((ancestors, size, width), kept),
            vmem((ancestors, size, width), kept),
            dma((12,)),
            dma((3, max(plane, ancestors))),
            dma((3, plane)),
            dma((3, plane)),
            dma((plane, cols)),
            dma((2, plane, cols)),
            dma((plane,)),
            dma((plane,)),
            dma((7,)),
            dma((7,)),
            dma((2, ancestors)),
            dma((2, ancestors)),
            dma((7, ancestors)),
            dma((7, ancestors)),
        ],
        compiler_params=pltpu.CompilerParams(
            collective_id=0, has_side_effects=True, vmem_limit_bytes=62 * 1024 * 1024
        ),
        name="fused_solve",
    )(
        block_col[0, 0, 0],
        block_row[0, 0, 0],
        block_count,
        leaf_rhs[0, 0, 0, 0],
        leaf_inv[0, 0, 0, 0],
        leaf_blocks[0, 0, 0],
        mid_rhs[0, 0, 0],
        mid_inv[0, 0, 0],
        anc_blocks[0, 0, 0],
        anc_rhs,
        anc_inv,
        anc_lower,
    )
    leaf_sol, mid_sol, anc_sol = pl.pallas_call(
        place_results,
        out_shape=[
            jax.ShapeDtypeStruct(value.shape, kept) for value in (leaf_sol, mid_sol, anc_sol)
        ],
        in_specs=[hbm] * 3,
        out_specs=[hbm] * 3,
        scratch_shapes=[dma((2 + ancestors,))],
        compiler_params=pltpu.CompilerParams(vmem_limit_bytes=62 * 1024 * 1024),
        name="place_results",
    )(leaf_sol, mid_sol, anc_sol)
    return (leaf_sol[None, None, None, None], mid_sol[None, None, None], anc_sol)


def fits_fused(mesh, rhs_count):
    layers, rows, cols = (mesh.shape[name] for name in ("layer", "row", "col"))
    pairs = layers == 2 and rows == 4 and cols % 2 == 0
    return pairs and rhs_count % (layers * rows * 128) == 0


def solution(mesh):
    in_specs = (
        P("layer", "row", "col", None, None, None),
        P("layer", "row", "col", None, None, None),
        P("layer", "row", "col", None, None, None),
        P("layer", "row", "col", None),
        P("layer", "row", "col", None),
        P("layer", "row", "col"),
        P("layer", "row", "col", None, None),
        P("layer", "row", "col", None, None),
        P("layer", "row", "col", None, None, None),
        P(),
        P(),
        P(),
    )
    out_specs = (
        P("layer", "row", "col", None, None, None),
        P("layer", "row", "col", None, None),
        P(),
    )

    def run(leaf_rhs, *rest):
        chosen = body
        if fits_fused(mesh, leaf_rhs.shape[-1]) and leaf_rhs.shape[3] == 1:
            sizes = (mesh.shape[name] for name in ("layer", "row", "col"))
            chosen = functools.partial(fused_body, *sizes)
        return jax.shard_map(
            chosen, mesh=mesh, in_specs=in_specs, out_specs=out_specs, check_vma=False
        )(leaf_rhs, *rest)

    return run
```

```python
import functools

import jax
import jax.numpy as jnp
from jax import lax
from jax.experimental import pallas as pl
from jax.experimental.pallas import tpu as pltpu
from jax.sharding import PartitionSpec as P

MESH = pl.DeviceIdType.MESH
LAG = 4


def solve_ancestors(partial_rows, rhs_rows, anc_inv, anc_lower):
    solved = []
    for anc_index in range(anc_inv.shape[0]):
        running = rhs_rows[anc_index].astype(jnp.float32) - partial_rows[anc_index]
        if anc_index > 0:
            offset = anc_index * (anc_index - 1) // 2
            earlier = anc_lower[offset : offset + anc_index]
            running = running - jnp.einsum(
                "bsj,bjt->st", earlier, jnp.stack(solved), preferred_element_type=jnp.float32
            )
        residue = running.astype(jnp.bfloat16)
        solved.append(
            jnp.dot(anc_inv[anc_index], residue, preferred_element_type=jnp.float32).astype(
                jnp.bfloat16
            )
        )
    return jnp.stack(solved)


def add_slots(received):
    return jnp.sum(received, axis=0)


def body(
    leaf_rhs,
    leaf_inv,
    leaf_blocks,
    block_col,
    block_row,
    block_count,
    mid_rhs,
    mid_inv,
    anc_blocks,
    anc_rhs,
    anc_inv,
    anc_lower,
):
    leaf_sol = jnp.einsum(
        "ksj,kjt->kst", leaf_inv[0, 0, 0], leaf_rhs[0, 0, 0], preferred_element_type=jnp.float32
    ).astype(jnp.bfloat16)
    factor_blocks = leaf_blocks[0, 0, 0]
    columns = block_col[0, 0, 0]
    targets = block_row[0, 0, 0]
    live_count = block_count[0, 0, 0]
    grid_cols = lax.axis_size("col")
    empty_term = jnp.zeros((grid_cols,) + leaf_sol.shape[1:], jnp.float32)
    piece = lax.all_gather(leaf_sol, "row", axis=0, tiled=True)
    piece_rows = piece.shape[0]

    def one_block(slot_index, current_sum):
        column = columns[slot_index]
        inside = (column >= 0) & (column < piece_rows)

        def add_one(partial_sum):
            chosen = lax.dynamic_index_in_dim(
                piece, jnp.clip(column, 0, piece_rows - 1), 0, keepdims=False
            )
            product = jnp.dot(factor_blocks[slot_index], chosen, preferred_element_type=jnp.float32)
            row_now = lax.dynamic_index_in_dim(partial_sum, targets[slot_index], 0, keepdims=False)
            return lax.dynamic_update_index_in_dim(
                partial_sum, row_now + product, targets[slot_index], 0
            )

        return lax.cond(inside, add_one, lambda unchanged: unchanged, current_sum)

    mid_terms = lax.fori_loop(0, live_count, one_block, empty_term)
    mid_own = add_slots(lax.all_to_all(mid_terms, "col", split_axis=0, concat_axis=0, tiled=True))
    residue = (mid_rhs[0, 0, 0].astype(jnp.float32) - mid_own).astype(jnp.bfloat16)
    mid_sol = jnp.dot(mid_inv[0, 0, 0], residue, preferred_element_type=jnp.float32).astype(
        jnp.bfloat16
    )
    anc_term = jnp.einsum(
        "asj,jt->ast", anc_blocks[0, 0, 0], mid_sol, preferred_element_type=jnp.float32
    )
    anc_part = lax.psum(anc_term, ("layer", "row", "col"))
    anc_sol = solve_ancestors(anc_part, anc_rhs, anc_inv, anc_lower)
    return (leaf_sol[None, None, None], mid_sol[None, None, None], anc_sol)


def fused_kernel(
    layers,
    rows,
    cols,
    block_col_h,
    block_row_h,
    block_count_h,
    leaf_rhs_h,
    leaf_inv_h,
    blocks_h,
    mid_rhs_h,
    mid_inv_h,
    anc_blocks_h,
    anc_rhs_h,
    anc_inv_h,
    anc_lower_h,
    leaf_out,
    mid_out,
    anc_out,
    block_col,
    block_row,
    block_count,
    leaf_rhs,
    leaf_inv,
    blocks,
    mid_rhs,
    mid_inv,
    anc_rhs,
    anc_inv,
    anc_lower,
    xs,
    dense,
    from_left,
    from_right,
    outgoing,
    acc,
    mid_own,
    mids,
    ancb,
    part_out,
    part_outer,
    part_inner,
    total,
    sol,
    load_sem,
    store_sem,
    a_send,
    a_recv,
    b_send,
    b_recv,
    m_send,
    m_recv,
    g_send,
    g_recv,
    c_send,
    c_recv,
    s_send,
    s_recv,
):
    layer, row, col = (lax.axis_index(name) for name in ("layer", "row", "col"))
    plane = layers * rows
    size, width = mid_own.shape[1:]
    ancestors = sol.shape[0]
    max_blocks = blocks.shape[0]
    half = cols // 2
    sib_row = (row // 2) * 2 + 1 - row % 2
    far_row = (row + rows // 2) % rows
    far_sib_row = (far_row // 2) * 2 + 1 - far_row % 2
    other = (layer + 1) % layers
    sib, across, far = (layer, sib_row, col), (other, row, col), (layer, far_row, col)

    def slot(of_layer, of_row):
        return of_layer * rows + of_row

    me = slot(layer, row)

    def remote(src, dst, send_sem, recv_sem, device):
        return pltpu.make_async_remote_copy(
            src_ref=src,
            dst_ref=dst,
            send_sem=send_sem,
            recv_sem=recv_sem,
            device_id=device,
            device_id_type=MESH,
        )

    def lanes(index):
        return pl.ds(pl.multiple_of(index * width, width), width)

    def depth_of(which):
        return pl.ds(pl.multiple_of(which * size, size), size)

    loads = [
        pltpu.make_async_copy(src, dst, load_sem.at[i])
        for i, (src, dst) in enumerate(
            [
                (leaf_inv_h, leaf_inv),
                (leaf_rhs_h, leaf_rhs),
                (anc_blocks_h, ancb.at[:, :, depth_of(me)]),
                (blocks_h, blocks),
                (mid_rhs_h, mid_rhs),
                (mid_inv_h, mid_inv),
                (anc_rhs_h.at[:, :, lanes(me)], anc_rhs),
                (anc_inv_h, anc_inv),
                (anc_lower_h, anc_lower),
                (block_col_h, block_col),
                (block_row_h, block_row),
                (block_count_h, block_count),
            ]
        )
    ]
    for load in loads:
        load.start()

    barrier = pltpu.get_barrier_semaphore()
    for step in range(1, plane):
        peer = (me + step) % plane
        pl.semaphore_signal(
            barrier, inc=1, device_id=(peer // rows, peer % rows, col), device_id_type=MESH
        )

    @pl.when(col > 0)
    def _():
        pl.semaphore_signal(barrier, inc=1, device_id=(layer, row, col - 1), device_id_type=MESH)

    @pl.when(col < cols - 1)
    def _():
        pl.semaphore_signal(barrier, inc=1, device_id=(layer, row, col + 1), device_id_type=MESH)

    loads[0].wait()
    loads[1].wait()
    ends = (col == 0).astype(jnp.int32) + (col == cols - 1).astype(jnp.int32)
    pl.semaphore_wait(barrier, plane + 1 - ends)

    def leaf_chunk(j, kind):
        at_row = (row, row, far_row)[kind]
        to = (sib, far, sib)[kind]
        ref = xs.at[j, at_row]
        return remote(ref, ref, a_send.at[kind, j], a_recv.at[kind, j], to)

    def leaf_arrival(j, kind):
        at_row = (sib_row, far_row, far_sib_row)[kind]
        ref = xs.at[j, at_row]
        return remote(ref, ref, a_send.at[kind, j], a_recv.at[kind, j], sib)

    def leaf_store(j):
        return pltpu.make_async_copy(
            xs.at[j, row], leaf_out.at[:, lanes(j)], store_sem.at[0, j]
        )

    def leaf_step(j, carry):
        xs[j, row] = jnp.dot(
            leaf_inv[...], leaf_rhs[:, lanes(j)], preferred_element_type=jnp.float32
        ).astype(xs.dtype)
        leaf_chunk(j, 1).start()
        leaf_chunk(j, 0).start()
        leaf_store(j).start()
        return carry

    lax.fori_loop(0, plane, leaf_step, 0)

    def block_copy(kind):
        which = (me, me, me, slot(other, row), slot(layer, far_row), slot(layer, far_row))
        which = (which + (slot(other, far_row),))[kind]
        to = (sib, across, far, sib, sib, across, sib)[kind]
        ref = ancb.at[:, :, depth_of(which)]
        return remote(ref, ref, g_send.at[kind], g_recv.at[kind], to)

    def block_arrival(kind):
        which = (
            slot(layer, sib_row),
            slot(other, row),
            slot(layer, far_row),
            slot(other, sib_row),
            slot(layer, far_sib_row),
            slot(other, far_row),
            slot(other, far_sib_row),
        )[kind]
        ref = ancb.at[:, :, depth_of(which)]
        return remote(ref, ref, g_send.at[kind], g_recv.at[kind], sib)

    loads[2].wait()
    block_copy(1).start()
    block_copy(2).start()
    block_copy(0).start()

    for load in loads[9:] + loads[3:4]:
        load.wait()

    def place_target(m, carry):
        for i in range(rows):
            found = jnp.int32(max_blocks)
            for n in range(max_blocks):
                hit = (block_col[n] == i) & (block_row[n] == m) & (n < block_count[0, 0, 0])
                found = jnp.where(hit, n, found)
            there = found < max_blocks
            block = blocks[jnp.minimum(found, max_blocks - 1)]
            keep = jnp.full(block.shape, there.astype(jnp.int32)) > 0
            dense[m, :, i * size : (i + 1) * size] = jnp.where(
                keep, block.astype(jnp.float32), 0.0
            ).astype(dense.dtype)
        return carry

    lax.fori_loop(0, cols, place_target, 0)

    def gathered(j):
        return xs[j].reshape(rows * size, width)

    def sum_copy(j, m, buffer, to):
        return remote(outgoing.at[j, m], buffer.at[j, m], b_send.at[j, m], b_recv_of(buffer, j, m), to)

    def b_recv_of(buffer, j, m):
        return b_recv.at[0 if buffer is from_left else 1, j, m]

    def sums_on(j, m, buffer, has_more, to):
        outgoing_sum = jnp.dot(dense[m], gathered(j), preferred_element_type=jnp.float32)

        @pl.when(has_more)
        def _():
            sum_copy(j, m, buffer, to).wait_recv()
            outgoing[j, m] = (outgoing_sum + buffer[j, m].astype(jnp.float32)).astype(
                outgoing.dtype
            )

        @pl.when(jnp.logical_not(has_more))
        def _():
            outgoing[j, m] = outgoing_sum.astype(outgoing.dtype)

        sum_copy(j, m, buffer, to).start()

    def mid_copy(j):
        return remote(
            mid_own.at[j], mids.at[me], m_send.at[j], m_recv.at[me], (j // rows, j % rows, col)
        )

    def mid_store(j):
        return pltpu.make_async_copy(mid_own.at[j], mid_out.at[:, lanes(j)], store_sem.at[1, j])

    def forward_leaf(j):
        leaf_arrival(j, 1).wait_recv()
        leaf_chunk(j, 2).start()

    loads[4].wait()
    loads[5].wait()
    forward_leaf(0)

    def sum_step(j, carry):
        @pl.when(j < plane)
        def _():
            @pl.when(j < plane - 1)
            def _():
                forward_leaf(j + 1)

            leaf_arrival(j, 0).wait_recv()
            leaf_arrival(j, 2).wait_recv()
            for distance in range(cols - 1, 0, -1):

                @pl.when(col + distance < cols)
                def _():
                    sums_on(j, col + distance, from_left, col > 0, (layer, row, col + 1))

                @pl.when(col - distance >= 0)
                def _():
                    sums_on(j, col - distance, from_right, col < cols - 1, (layer, row, col - 1))

        @pl.when(j == 3)
        def _():
            block_arrival(1).wait_recv()
            block_copy(3).start()

        @pl.when(j == 6)
        def _():
            block_arrival(2).wait_recv()
            block_copy(5).start()
            block_copy(4).start()

        @pl.when(j >= LAG)
        def _():
            done = j - LAG
            acc[...] = mid_rhs[:, lanes(done)].astype(jnp.float32) - jnp.dot(
                dense[col], gathered(done), preferred_element_type=jnp.float32
            )

            @pl.when(col > 0)
            def _():
                sum_copy(done, col, from_left, sib).wait_recv()
                acc[...] -= from_left[done, col].astype(jnp.float32)

            @pl.when(col < cols - 1)
            def _():
                sum_copy(done, col, from_right, sib).wait_recv()
                acc[...] -= from_right[done, col].astype(jnp.float32)

            solved = jnp.dot(
                mid_inv[...], acc[...].astype(jnp.bfloat16), preferred_element_type=jnp.float32
            ).astype(jnp.bfloat16)
            mid_own[done] = solved

            @pl.when(done == me)
            def _():
                mids[me] = solved

            @pl.when(done != me)
            def _():
                mid_copy(done).start()

            mid_store(done).start()

        return carry

    lax.fori_loop(0, plane + LAG, sum_step, 0)

    block_arrival(5).wait_recv()
    block_copy(6).start()
    for kind in (0, 3, 4, 6):
        block_arrival(kind).wait_recv()
    for step in range(1, plane):
        peer = (me + step) % plane
        remote(mids.at[peer], mids.at[peer], m_send.at[0], m_recv.at[peer], sib).wait_recv()
    for load in loads[6:9]:
        load.wait()

    in_left = col < half
    inward = (layer, row, jnp.where(in_left, col + 1, col - 1))
    outward = (layer, row, jnp.where(in_left, col - 1, col + 1))
    middle = (col == half - 1) | (col == half)
    has_outer = (col > 0) & (col < cols - 1)

    def up_copy(a, buffer, kind, to):
        return remote(part_out.at[a], buffer.at[a], c_send.at[0, a], c_recv.at[kind, a], to)

    def down_copy(a):
        return remote(total.at[a], part_inner.at[a], c_send.at[1, a], c_recv.at[1, a], outward)

    def sum_up(a):
        acc[...] = jnp.dot(
            ancb[a], mids[...].reshape(plane * size, width), preferred_element_type=jnp.float32
        )

        @pl.when(has_outer)
        def _():
            up_copy(a, part_outer, 0, sib).wait_recv()
            acc[...] += part_outer[a].astype(jnp.float32)

        part_out[a] = acc[...].astype(part_out.dtype)

        @pl.when(middle)
        def _():
            up_copy(a, part_inner, 1, inward).start()

        @pl.when(jnp.logical_not(middle))
        def _():
            up_copy(a, part_outer, 0, inward).start()

    def sol_ref(a, which):
        return anc_out.at[a, :, lanes(which)]

    def sol_copy(a, kind):
        turn = a % 2
        which = (
            me,
            me,
            me,
            slot(other, row),
            slot(layer, far_row),
            (slot(other, row), slot(layer, far_row))[turn],
            slot(other, far_row),
        )[kind]
        to = (sib, across, far, sib, sib, (far, across)[turn], sib)[kind]
        src = sol.at[a] if kind < 3 else sol_ref(a, which)
        return remote(src, sol_ref(a, which), s_send.at[kind, a], s_recv.at[kind, a], to)

    def sol_arrival(a, kind):
        which = (
            slot(layer, sib_row),
            slot(other, row),
            slot(layer, far_row),
            slot(other, sib_row),
            slot(layer, far_sib_row),
            slot(other, far_row),
            slot(other, far_sib_row),
        )[kind]
        return remote(sol.at[a], sol_ref(a, which), s_send.at[kind, a], s_recv.at[kind, a], sib)

    def sol_store(a):
        return pltpu.make_async_copy(sol.at[a], sol_ref(a, me), store_sem.at[2, a])

    def solve_down(a):
        up_copy(a, part_inner, 1, sib).wait_recv()

        @pl.when(middle)
        def _():
            total[a] = (
                part_out[a].astype(jnp.float32) + part_inner[a].astype(jnp.float32)
            ).astype(total.dtype)

        @pl.when(jnp.logical_not(middle))
        def _():
            total[a] = part_inner[a]

        @pl.when(has_outer)
        def _():
            down_copy(a).start()

        running = anc_rhs[a].astype(jnp.float32) - total[a].astype(jnp.float32)
        offset = a * (a - 1) // 2
        for b in range(a):
            running -= jnp.dot(anc_lower[offset + b], sol[b], preferred_element_type=jnp.float32)
        sol[a] = jnp.dot(
            anc_inv[a], running.astype(jnp.bfloat16), preferred_element_type=jnp.float32
        ).astype(sol.dtype)
        for kind in (2, 1, 0):
            sol_copy(a, kind).start()
        sol_store(a).start()

    def relay(a):
        for kind in ((1, 2), (2, 1))[a % 2]:
            sol_arrival(a, kind).wait_recv()
            if kind == 1 + a % 2:
                sol_copy(a, 5).start()
            sol_copy(a, kind + 2).start()
    for a in range(ancestors + 3):
        if a < ancestors:
            sum_up(a)
        if 2 <= a < ancestors + 2:
            solve_down(a - 2)
        if a >= 3:
            relay(a - 3)
    for a in range(ancestors):
        sol_arrival(a, 5).wait_recv()
        sol_copy(a, 6).start()

    def drain(j, carry):
        for kind in range(3):
            leaf_chunk(j, kind).wait_send()
        leaf_store(j).wait()
        mid_store(j).wait()

        @pl.when(j != me)
        def _():
            mid_copy(j).wait_send()

        def drain_sums(m, inner):
            @pl.when(m != col)
            def _():
                sum_copy(j, m, from_left, sib).wait_send()

            return inner

        lax.fori_loop(0, cols, drain_sums, 0)
        return carry

    lax.fori_loop(0, plane, drain, 0)
    for kind in range(7):
        block_copy(kind).wait_send()
    for a in range(ancestors):
        up_copy(a, part_inner, 1, sib).wait_send()

        @pl.when(has_outer)
        def _():
            down_copy(a).wait_send()

        for kind in range(7):
            sol_copy(a, kind).wait_send()
        sol_store(a).wait()
        for kind in (0, 3, 4, 6):
            sol_arrival(a, kind).wait_recv()


def place_results(leaf_in, mid_in, anc_in, leaf_out, mid_out, anc_out, held, anc_held, sem):
    ancestors = anc_in.shape[0]
    parts = [(anc_in.at[a], anc_held.at[a], anc_out.at[a]) for a in range(ancestors)]
    parts.append((leaf_in, held.at[0], leaf_out))
    parts.append((mid_in, held.at[1], mid_out))
    reads = [pltpu.make_async_copy(a, b, sem.at[0, i]) for i, (a, b, _) in enumerate(parts)]
    writes = [pltpu.make_async_copy(b, c, sem.at[1, i]) for i, (_, b, c) in enumerate(parts)]
    for read in reads:
        read.start()
    for read, write in zip(reads, writes):
        read.wait()
        write.start()
    for write in writes:
        write.wait()


def fused_body(
    layers,
    rows,
    cols,
    leaf_rhs,
    leaf_inv,
    leaf_blocks,
    block_col,
    block_row,
    block_count,
    mid_rhs,
    mid_inv,
    anc_blocks,
    anc_rhs,
    anc_inv,
    anc_lower,
):
    plane = layers * rows
    size, rhs_count = mid_rhs.shape[-2:]
    ancestors = anc_inv.shape[0]
    max_blocks = leaf_blocks.shape[3]
    width = rhs_count // plane
    kept = mid_rhs.dtype
    anywhere = pl.BlockSpec(memory_space=pl.ANY)
    hbm = pl.BlockSpec(memory_space=pltpu.HBM)
    dma = pltpu.SemaphoreType.DMA
    vmem = pltpu.VMEM
    leaf_sol, mid_sol, anc_sol = pl.pallas_call(
        functools.partial(fused_kernel, layers, rows, cols),
        out_shape=[
            jax.ShapeDtypeStruct((size, rhs_count), kept),
            jax.ShapeDtypeStruct((size, rhs_count), kept),
            jax.ShapeDtypeStruct((ancestors, size, rhs_count), kept),
        ],
        in_specs=[hbm] * 12,
        out_specs=[anywhere] * 3,
        scratch_shapes=[
            pltpu.SMEM((max_blocks,), jnp.int32),
            pltpu.SMEM((max_blocks,), jnp.int32),
            pltpu.SMEM(block_count.shape, jnp.int32),
            vmem((size, rhs_count), kept),
            vmem((size, size), kept),
            vmem((max_blocks, size, size), kept),
            vmem((size, rhs_count), kept),
            vmem((size, size), kept),
            vmem((ancestors, size, width), kept),
            vmem(anc_inv.shape, kept),
            vmem(anc_lower.shape, kept),
            vmem((plane, rows, size, width), kept),
            vmem((cols, size, rows * size), kept),
            vmem((plane, cols, size, width), kept),
            vmem((plane, cols, size, width), kept),
            vmem((plane, cols, size, width), kept),
            vmem((size, width), jnp.float32),
            vmem((plane, size, width), kept),
            vmem((plane, size, width), kept),
            vmem((ancestors, size, plane * size), kept),
            vmem((ancestors, size, width), kept),
            vmem((ancestors, size, width), kept),
            vmem((ancestors, size, width), kept),
            vmem((ancestors, size, width), kept),
            vmem((ancestors, size, width), kept),
            dma((12,)),
            dma((3, max(plane, ancestors))),
            dma((3, plane)),
            dma((3, plane)),
            dma((plane, cols)),
            dma((2, plane, cols)),
            dma((plane,)),
            dma((plane,)),
            dma((7,)),
            dma((7,)),
            dma((2, ancestors)),
            dma((2, ancestors)),
            dma((7, ancestors)),
            dma((7, ancestors)),
        ],
        compiler_params=pltpu.CompilerParams(
            collective_id=0, has_side_effects=True, vmem_limit_bytes=62 * 1024 * 1024
        ),
        name="fused_solve",
    )(
        block_col[0, 0, 0],
        block_row[0, 0, 0],
        block_count,
        leaf_rhs[0, 0, 0, 0],
        leaf_inv[0, 0, 0, 0],
        leaf_blocks[0, 0, 0],
        mid_rhs[0, 0, 0],
        mid_inv[0, 0, 0],
        anc_blocks[0, 0, 0],
        anc_rhs,
        anc_inv,
        anc_lower,
    )
    leaf_sol, mid_sol, anc_sol = pl.pallas_call(
        place_results,
        out_shape=[
            jax.ShapeDtypeStruct(value.shape, kept) for value in (leaf_sol, mid_sol, anc_sol)
        ],
        in_specs=[hbm] * 3,
        out_specs=[hbm] * 3,
        scratch_shapes=[
            vmem((2, size, rhs_count), kept),
            vmem(anc_sol.shape, kept),
            dma((2, 2 + ancestors)),
        ],
        compiler_params=pltpu.CompilerParams(vmem_limit_bytes=62 * 1024 * 1024),
        name="place_results",
    )(leaf_sol, mid_sol, anc_sol)
    return (leaf_sol[None, None, None, None], mid_sol[None, None, None], anc_sol)


def fits_fused(mesh, rhs_count):
    layers, rows, cols = (mesh.shape[name] for name in ("layer", "row", "col"))
    pairs = layers == 2 and rows == 4 and cols % 2 == 0
    return pairs and rhs_count % (layers * rows * 128) == 0


def solution(mesh):
    in_specs = (
        P("layer", "row", "col", None, None, None),
        P("layer", "row", "col", None, None, None),
        P("layer", "row", "col", None, None, None),
        P("layer", "row", "col", None),
        P("layer", "row", "col", None),
        P("layer", "row", "col"),
        P("layer", "row", "col", None, None),
        P("layer", "row", "col", None, None),
        P("layer", "row", "col", None, None, None),
        P(),
        P(),
        P(),
    )
    out_specs = (
        P("layer", "row", "col", None, None, None),
        P("layer", "row", "col", None, None),
        P(),
    )

    def run(leaf_rhs, *rest):
        chosen = body
        if fits_fused(mesh, leaf_rhs.shape[-1]) and leaf_rhs.shape[3] == 1:
            sizes = (mesh.shape[name] for name in ("layer", "row", "col"))
            chosen = functools.partial(fused_body, *sizes)
        return jax.shard_map(
            chosen, mesh=mesh, in_specs=in_specs, out_specs=out_specs, check_vma=False
        )(leaf_rhs, *rest)

    return run
```

```python
import functools

import jax
import jax.numpy as jnp
from jax import lax
from jax.experimental import pallas as pl
from jax.experimental.pallas import tpu as pltpu
from jax.sharding import PartitionSpec as P

MESH = pl.DeviceIdType.MESH
LAG_END, LAG_INSIDE = 7, 3


def solve_ancestors(partial_rows, rhs_rows, anc_inv, anc_lower):
    solved = []
    for anc_index in range(anc_inv.shape[0]):
        running = rhs_rows[anc_index].astype(jnp.float32) - partial_rows[anc_index]
        if anc_index > 0:
            offset = anc_index * (anc_index - 1) // 2
            earlier = anc_lower[offset : offset + anc_index]
            running = running - jnp.einsum(
                "bsj,bjt->st", earlier, jnp.stack(solved), preferred_element_type=jnp.float32
            )
        residue = running.astype(jnp.bfloat16)
        solved.append(
            jnp.dot(anc_inv[anc_index], residue, preferred_element_type=jnp.float32).astype(
                jnp.bfloat16
            )
        )
    return jnp.stack(solved)


def add_slots(received):
    return jnp.sum(received, axis=0)


def body(
    leaf_rhs,
    leaf_inv,
    leaf_blocks,
    block_col,
    block_row,
    block_count,
    mid_rhs,
    mid_inv,
    anc_blocks,
    anc_rhs,
    anc_inv,
    anc_lower,
):
    leaf_sol = jnp.einsum(
        "ksj,kjt->kst", leaf_inv[0, 0, 0], leaf_rhs[0, 0, 0], preferred_element_type=jnp.float32
    ).astype(jnp.bfloat16)
    factor_blocks = leaf_blocks[0, 0, 0]
    columns = block_col[0, 0, 0]
    targets = block_row[0, 0, 0]
    live_count = block_count[0, 0, 0]
    grid_cols = lax.axis_size("col")
    empty_term = jnp.zeros((grid_cols,) + leaf_sol.shape[1:], jnp.float32)
    piece = lax.all_gather(leaf_sol, "row", axis=0, tiled=True)
    piece_rows = piece.shape[0]

    def one_block(slot_index, current_sum):
        column = columns[slot_index]
        inside = (column >= 0) & (column < piece_rows)

        def add_one(partial_sum):
            chosen = lax.dynamic_index_in_dim(
                piece, jnp.clip(column, 0, piece_rows - 1), 0, keepdims=False
            )
            product = jnp.dot(factor_blocks[slot_index], chosen, preferred_element_type=jnp.float32)
            row_now = lax.dynamic_index_in_dim(partial_sum, targets[slot_index], 0, keepdims=False)
            return lax.dynamic_update_index_in_dim(
                partial_sum, row_now + product, targets[slot_index], 0
            )

        return lax.cond(inside, add_one, lambda unchanged: unchanged, current_sum)

    mid_terms = lax.fori_loop(0, live_count, one_block, empty_term)
    mid_own = add_slots(lax.all_to_all(mid_terms, "col", split_axis=0, concat_axis=0, tiled=True))
    residue = (mid_rhs[0, 0, 0].astype(jnp.float32) - mid_own).astype(jnp.bfloat16)
    mid_sol = jnp.dot(mid_inv[0, 0, 0], residue, preferred_element_type=jnp.float32).astype(
        jnp.bfloat16
    )
    anc_term = jnp.einsum(
        "asj,jt->ast", anc_blocks[0, 0, 0], mid_sol, preferred_element_type=jnp.float32
    )
    anc_part = lax.psum(anc_term, ("layer", "row", "col"))
    anc_sol = solve_ancestors(anc_part, anc_rhs, anc_inv, anc_lower)
    return (leaf_sol[None, None, None], mid_sol[None, None, None], anc_sol)


def fused_kernel(
    layers,
    rows,
    cols,
    block_col_h,
    block_row_h,
    block_count_h,
    leaf_rhs_h,
    leaf_inv_h,
    blocks_h,
    mid_rhs_h,
    mid_inv_h,
    anc_blocks_h,
    anc_rhs_h,
    anc_inv_h,
    anc_lower_h,
    leaf_out,
    mid_out,
    anc_out,
    block_col,
    block_row,
    block_count,
    leaf_rhs,
    leaf_inv,
    blocks,
    mid_rhs,
    mid_inv,
    anc_rhs,
    anc_inv,
    anc_lower,
    xs,
    dense,
    from_left,
    from_right,
    outgoing,
    acc,
    terms,
    own_terms,
    mid_own,
    mids,
    ancb,
    part_out,
    part_outer,
    part_inner,
    total,
    sol,
    load_sem,
    store_sem,
    a_send,
    a_recv,
    b_send,
    b_recv,
    m_send,
    m_recv,
    g_send,
    g_recv,
    c_send,
    c_recv,
    s_send,
    s_recv,
):
    layer, row, col = (lax.axis_index(name) for name in ("layer", "row", "col"))
    plane = layers * rows
    size, width = mid_own.shape[1:]
    ancestors = sol.shape[0]
    max_blocks = blocks.shape[0]
    half = cols // 2
    sib_row = (row // 2) * 2 + 1 - row % 2
    far_row = (row + rows // 2) % rows
    far_sib_row = (far_row // 2) * 2 + 1 - far_row % 2
    other = (layer + 1) % layers
    sib, across, far = (layer, sib_row, col), (other, row, col), (layer, far_row, col)

    def slot(of_layer, of_row):
        return of_layer * rows + of_row

    me = slot(layer, row)

    def remote(src, dst, send_sem, recv_sem, device):
        return pltpu.make_async_remote_copy(
            src_ref=src,
            dst_ref=dst,
            send_sem=send_sem,
            recv_sem=recv_sem,
            device_id=device,
            device_id_type=MESH,
        )

    def lanes(index):
        return pl.ds(pl.multiple_of(index * width, width), width)

    def depth_of(which):
        return pl.ds(pl.multiple_of(which * size, size), size)

    loads = [
        pltpu.make_async_copy(src, dst, load_sem.at[i])
        for i, (src, dst) in enumerate(
            [
                (leaf_inv_h, leaf_inv),
                (leaf_rhs_h, leaf_rhs),
                (anc_blocks_h, ancb.at[:, :, depth_of(me)]),
                (blocks_h, blocks),
                (mid_rhs_h, mid_rhs),
                (mid_inv_h, mid_inv),
                (anc_rhs_h.at[:, :, lanes(me)], anc_rhs),
                (anc_inv_h, anc_inv),
                (anc_lower_h, anc_lower),
                (block_col_h, block_col),
                (block_row_h, block_row),
                (block_count_h, block_count),
            ]
        )
    ]
    for load in loads:
        load.start()

    barrier = pltpu.get_barrier_semaphore()
    for step in range(1, plane):
        peer = (me + step) % plane
        pl.semaphore_signal(
            barrier, inc=1, device_id=(peer // rows, peer % rows, col), device_id_type=MESH
        )

    @pl.when(col > 0)
    def _():
        pl.semaphore_signal(barrier, inc=1, device_id=(layer, row, col - 1), device_id_type=MESH)

    @pl.when(col < cols - 1)
    def _():
        pl.semaphore_signal(barrier, inc=1, device_id=(layer, row, col + 1), device_id_type=MESH)

    loads[0].wait()
    loads[1].wait()
    ends = (col == 0).astype(jnp.int32) + (col == cols - 1).astype(jnp.int32)
    pl.semaphore_wait(barrier, plane + 1 - ends)

    def leaf_chunk(j, kind):
        at_row = (row, row, far_row)[kind]
        to = (sib, far, sib)[kind]
        ref = xs.at[j, at_row]
        return remote(ref, ref, a_send.at[kind, j], a_recv.at[kind, j], to)

    def leaf_arrival(j, kind):
        at_row = (sib_row, far_row, far_sib_row)[kind]
        ref = xs.at[j, at_row]
        return remote(ref, ref, a_send.at[kind, j], a_recv.at[kind, j], sib)

    def leaf_store(j):
        return pltpu.make_async_copy(
            xs.at[j, row], leaf_out.at[:, lanes(j)], store_sem.at[0, j]
        )

    def leaf_step(j, carry):
        xs[j, row] = jnp.dot(
            leaf_inv[...], leaf_rhs[:, lanes(j)], preferred_element_type=jnp.float32
        ).astype(xs.dtype)
        leaf_chunk(j, 1).start()
        leaf_chunk(j, 0).start()
        leaf_store(j).start()
        return carry

    lax.fori_loop(0, plane, leaf_step, 0)

    def block_copy(kind):
        which = (me, me, me, slot(other, row), slot(layer, far_row), slot(layer, far_row))
        which = (which + (slot(other, far_row),))[kind]
        to = (sib, across, far, sib, sib, across, sib)[kind]
        ref = ancb.at[:, :, depth_of(which)]
        return remote(ref, ref, g_send.at[kind], g_recv.at[kind], to)

    def block_arrival(kind):
        which = (
            slot(layer, sib_row),
            slot(other, row),
            slot(layer, far_row),
            slot(other, sib_row),
            slot(layer, far_sib_row),
            slot(other, far_row),
            slot(other, far_sib_row),
        )[kind]
        ref = ancb.at[:, :, depth_of(which)]
        return remote(ref, ref, g_send.at[kind], g_recv.at[kind], sib)

    loads[2].wait()
    block_copy(1).start()
    block_copy(2).start()
    block_copy(0).start()

    for load in loads[9:] + loads[3:4]:
        load.wait()

    def place_target(m, carry):
        for i in range(rows):
            found = jnp.int32(max_blocks)
            for n in range(max_blocks):
                hit = (block_col[n] == i) & (block_row[n] == m) & (n < block_count[0, 0, 0])
                found = jnp.where(hit, n, found)
            there = found < max_blocks
            block = blocks[jnp.minimum(found, max_blocks - 1)]
            keep = jnp.full(block.shape, there.astype(jnp.int32)) > 0
            dense[m, :, i * size : (i + 1) * size] = jnp.where(
                keep, block.astype(jnp.float32), 0.0
            ).astype(dense.dtype)
        return carry

    lax.fori_loop(0, cols, place_target, 0)

    def gathered(j):
        return xs[j].reshape(rows * size, width)

    def sum_copy(j, m, buffer, to):
        return remote(outgoing.at[j, m], buffer.at[j, m], b_send.at[j, m], b_recv_of(buffer, j, m), to)

    def b_recv_of(buffer, j, m):
        return b_recv.at[0 if buffer is from_left else 1, j, m]

    def sums_on(j, m, buffer, has_more, to):
        outgoing_sum = terms[m]

        @pl.when(has_more)
        def _():
            sum_copy(j, m, buffer, to).wait_recv()
            outgoing[j, m] = (outgoing_sum + buffer[j, m].astype(jnp.float32)).astype(
                outgoing.dtype
            )

        @pl.when(jnp.logical_not(has_more))
        def _():
            outgoing[j, m] = outgoing_sum.astype(outgoing.dtype)

        sum_copy(j, m, buffer, to).start()

    def mid_copy(j):
        return remote(
            mid_own.at[j], mids.at[me], m_send.at[j], m_recv.at[me], (j // rows, j % rows, col)
        )

    def mid_store(j):
        return pltpu.make_async_copy(mid_own.at[j], mid_out.at[:, lanes(j)], store_sem.at[1, j])

    def forward_leaf(j):
        leaf_arrival(j, 1).wait_recv()
        leaf_chunk(j, 2).start()

    loads[4].wait()
    loads[5].wait()
    forward_leaf(0)
    lag = jnp.where((col == 0) | (col == cols - 1), LAG_END, LAG_INSIDE)

    def sum_step(j, carry):
        @pl.when(j < plane)
        def _():
            @pl.when(j < plane - 1)
            def _():
                forward_leaf(j + 1)

            leaf_arrival(j, 0).wait_recv()
            leaf_arrival(j, 2).wait_recv()
            terms[...] = jnp.dot(
                dense[...].reshape(cols * size, rows * size),
                gathered(j),
                preferred_element_type=jnp.float32,
            ).reshape(cols, size, width)
            own_terms[j] = terms[col]
            for distance in range(cols - 1, 0, -1):

                @pl.when(col + distance < cols)
                def _():
                    sums_on(j, col + distance, from_left, col > 0, (layer, row, col + 1))

                @pl.when(col - distance >= 0)
                def _():
                    sums_on(j, col - distance, from_right, col < cols - 1, (layer, row, col - 1))

        @pl.when(j == 3)
        def _():
            block_arrival(1).wait_recv()
            block_copy(3).start()

        @pl.when(j == 6)
        def _():
            block_arrival(2).wait_recv()
            block_copy(5).start()
            block_copy(4).start()

        @pl.when((j >= lag) & (j < plane + lag))
        def _():
            done = j - lag
            acc[...] = mid_rhs[:, lanes(done)].astype(jnp.float32) - own_terms[done]

            @pl.when(col > 0)
            def _():
                sum_copy(done, col, from_left, sib).wait_recv()
                acc[...] -= from_left[done, col].astype(jnp.float32)

            @pl.when(col < cols - 1)
            def _():
                sum_copy(done, col, from_right, sib).wait_recv()
                acc[...] -= from_right[done, col].astype(jnp.float32)

            solved = jnp.dot(
                mid_inv[...], acc[...].astype(jnp.bfloat16), preferred_element_type=jnp.float32
            ).astype(jnp.bfloat16)
            mid_own[done] = solved

            @pl.when(done == me)
            def _():
                mids[me] = solved

            @pl.when(done != me)
            def _():
                mid_copy(done).start()

            mid_store(done).start()

        return carry

    lax.fori_loop(0, plane + max(LAG_END, LAG_INSIDE), sum_step, 0)

    block_arrival(5).wait_recv()
    block_copy(6).start()
    for kind in (0, 3, 4, 6):
        block_arrival(kind).wait_recv()
    for step in range(1, plane):
        peer = (me + step) % plane
        remote(mids.at[peer], mids.at[peer], m_send.at[0], m_recv.at[peer], sib).wait_recv()
    for load in loads[6:9]:
        load.wait()

    in_left = col < half
    inward = (layer, row, jnp.where(in_left, col + 1, col - 1))
    outward = (layer, row, jnp.where(in_left, col - 1, col + 1))
    middle = (col == half - 1) | (col == half)
    has_outer = (col > 0) & (col < cols - 1)

    def up_copy(a, buffer, kind, to):
        return remote(part_out.at[a], buffer.at[a], c_send.at[0, a], c_recv.at[kind, a], to)

    def down_copy(a):
        return remote(total.at[a], part_inner.at[a], c_send.at[1, a], c_recv.at[1, a], outward)

    def sum_up(a):
        acc[...] = jnp.dot(
            ancb[a], mids[...].reshape(plane * size, width), preferred_element_type=jnp.float32
        )

        @pl.when(has_outer)
        def _():
            up_copy(a, part_outer, 0, sib).wait_recv()
            acc[...] += part_outer[a].astype(jnp.float32)

        part_out[a] = acc[...].astype(part_out.dtype)

        @pl.when(middle)
        def _():
            up_copy(a, part_inner, 1, inward).start()

        @pl.when(jnp.logical_not(middle))
        def _():
            up_copy(a, part_outer, 0, inward).start()

    def sol_ref(a, which):
        return anc_out.at[a, :, lanes(which)]

    def sol_copy(a, kind):
        turn = a % 2
        which = (
            me,
            me,
            me,
            slot(other, row),
            slot(layer, far_row),
            (slot(other, row), slot(layer, far_row))[turn],
            slot(other, far_row),
        )[kind]
        to = (sib, across, far, sib, sib, (far, across)[turn], sib)[kind]
        src = sol.at[a] if kind < 3 else sol_ref(a, which)
        return remote(src, sol_ref(a, which), s_send.at[kind, a], s_recv.at[kind, a], to)

    def sol_arrival(a, kind):
        which = (
            slot(layer, sib_row),
            slot(other, row),
            slot(layer, far_row),
            slot(other, sib_row),
            slot(layer, far_sib_row),
            slot(other, far_row),
            slot(other, far_sib_row),
        )[kind]
        return remote(sol.at[a], sol_ref(a, which), s_send.at[kind, a], s_recv.at[kind, a], sib)

    def sol_store(a):
        return pltpu.make_async_copy(sol.at[a], sol_ref(a, me), store_sem.at[2, a])

    def total_down(a, of_middle):
        @pl.when(middle if of_middle else jnp.logical_not(middle))
        def _():
            up_copy(a, part_inner, 1, sib).wait_recv()
            value = part_inner[a].astype(jnp.float32)
            if of_middle:
                value += part_out[a].astype(jnp.float32)
            total[a] = value.astype(total.dtype)

            @pl.when(has_outer)
            def _():
                down_copy(a).start()

    def solve(a):
        running = anc_rhs[a].astype(jnp.float32) - total[a].astype(jnp.float32)
        offset = a * (a - 1) // 2
        for b in range(a):
            running -= jnp.dot(anc_lower[offset + b], sol[b], preferred_element_type=jnp.float32)
        sol[a] = jnp.dot(
            anc_inv[a], running.astype(jnp.bfloat16), preferred_element_type=jnp.float32
        ).astype(sol.dtype)
        for kind in (2, 1, 0):
            sol_copy(a, kind).start()
        sol_store(a).start()

    def relay(a):
        for kind in ((1, 2), (2, 1))[a % 2]:
            sol_arrival(a, kind).wait_recv()
            if kind == 1 + a % 2:
                sol_copy(a, 5).start()
            sol_copy(a, kind + 2).start()
    for a in range(ancestors + 2):
        if a < ancestors:
            sum_up(a)
        if a >= 2:
            total_down(a - 2, True)
    for a in range(ancestors):
        total_down(a, False)
        solve(a)
    for a in range(ancestors):
        relay(a)
    for a in range(ancestors):
        sol_arrival(a, 5).wait_recv()
        sol_copy(a, 6).start()

    def drain(j, carry):
        for kind in range(3):
            leaf_chunk(j, kind).wait_send()
        leaf_store(j).wait()
        mid_store(j).wait()

        @pl.when(j != me)
        def _():
            mid_copy(j).wait_send()

        def drain_sums(m, inner):
            @pl.when(m != col)
            def _():
                sum_copy(j, m, from_left, sib).wait_send()

            return inner

        lax.fori_loop(0, cols, drain_sums, 0)
        return carry

    lax.fori_loop(0, plane, drain, 0)
    for kind in range(7):
        block_copy(kind).wait_send()
    for a in range(ancestors):
        up_copy(a, part_inner, 1, sib).wait_send()

        @pl.when(has_outer)
        def _():
            down_copy(a).wait_send()

        for kind in range(7):
            sol_copy(a, kind).wait_send()
        sol_store(a).wait()
        for kind in (0, 3, 4, 6):
            sol_arrival(a, kind).wait_recv()


def place_results(leaf_in, mid_in, anc_in, leaf_out, mid_out, anc_out, held, anc_held, sem):
    ancestors = anc_in.shape[0]
    parts = [(anc_in.at[a], anc_held.at[a], anc_out.at[a]) for a in range(ancestors)]
    parts.append((leaf_in, held.at[0], leaf_out))
    parts.append((mid_in, held.at[1], mid_out))
    reads = [pltpu.make_async_copy(a, b, sem.at[0, i]) for i, (a, b, _) in enumerate(parts)]
    writes = [pltpu.make_async_copy(b, c, sem.at[1, i]) for i, (_, b, c) in enumerate(parts)]
    for read in reads:
        read.start()
    for read, write in zip(reads, writes):
        read.wait()
        write.start()
    for write in writes:
        write.wait()


def fused_body(
    layers,
    rows,
    cols,
    leaf_rhs,
    leaf_inv,
    leaf_blocks,
    block_col,
    block_row,
    block_count,
    mid_rhs,
    mid_inv,
    anc_blocks,
    anc_rhs,
    anc_inv,
    anc_lower,
):
    plane = layers * rows
    size, rhs_count = mid_rhs.shape[-2:]
    ancestors = anc_inv.shape[0]
    max_blocks = leaf_blocks.shape[3]
    width = rhs_count // plane
    kept = mid_rhs.dtype
    anywhere = pl.BlockSpec(memory_space=pl.ANY)
    hbm = pl.BlockSpec(memory_space=pltpu.HBM)
    dma = pltpu.SemaphoreType.DMA
    vmem = pltpu.VMEM
    leaf_sol, mid_sol, anc_sol = pl.pallas_call(
        functools.partial(fused_kernel, layers, rows, cols),
        out_shape=[
            jax.ShapeDtypeStruct((size, rhs_count), kept),
            jax.ShapeDtypeStruct((size, rhs_count), kept),
            jax.ShapeDtypeStruct((ancestors, size, rhs_count), kept),
        ],
        in_specs=[hbm] * 12,
        out_specs=[anywhere] * 3,
        scratch_shapes=[
            pltpu.SMEM((max_blocks,), jnp.int32),
            pltpu.SMEM((max_blocks,), jnp.int32),
            pltpu.SMEM(block_count.shape, jnp.int32),
            vmem((size, rhs_count), kept),
            vmem((size, size), kept),
            vmem((max_blocks, size, size), kept),
            vmem((size, rhs_count), kept),
            vmem((size, size), kept),
            vmem((ancestors, size, width), kept),
            vmem(anc_inv.shape, kept),
            vmem(anc_lower.shape, kept),
            vmem((plane, rows, size, width), kept),
            vmem((cols, size, rows * size), kept),
            vmem((plane, cols, size, width), kept),
            vmem((plane, cols, size, width), kept),
            vmem((plane, cols, size, width), kept),
            vmem((size, width), jnp.float32),
            vmem((cols, size, width), jnp.float32),
            vmem((plane, size, width), jnp.float32),
            vmem((plane, size, width), kept),
            vmem((plane, size, width), kept),
            vmem((ancestors, size, plane * size), kept),
            vmem((ancestors, size, width), kept),
            vmem((ancestors, size, width), kept),
            vmem((ancestors, size, width), kept),
            vmem((ancestors, size, width), kept),
            vmem((ancestors, size, width), kept),
            dma((12,)),
            dma((3, max(plane, ancestors))),
            dma((3, plane)),
            dma((3, plane)),
            dma((plane, cols)),
            dma((2, plane, cols)),
            dma((plane,)),
            dma((plane,)),
            dma((7,)),
            dma((7,)),
            dma((2, ancestors)),
            dma((2, ancestors)),
            dma((7, ancestors)),
            dma((7, ancestors)),
        ],
        compiler_params=pltpu.CompilerParams(
            collective_id=0, has_side_effects=True, vmem_limit_bytes=62 * 1024 * 1024
        ),
        name="fused_solve",
    )(
        block_col[0, 0, 0],
        block_row[0, 0, 0],
        block_count,
        leaf_rhs[0, 0, 0, 0],
        leaf_inv[0, 0, 0, 0],
        leaf_blocks[0, 0, 0],
        mid_rhs[0, 0, 0],
        mid_inv[0, 0, 0],
        anc_blocks[0, 0, 0],
        anc_rhs,
        anc_inv,
        anc_lower,
    )
    leaf_sol, mid_sol, anc_sol = pl.pallas_call(
        place_results,
        out_shape=[
            jax.ShapeDtypeStruct(value.shape, kept) for value in (leaf_sol, mid_sol, anc_sol)
        ],
        in_specs=[hbm] * 3,
        out_specs=[hbm] * 3,
        scratch_shapes=[
            vmem((2, size, rhs_count), kept),
            vmem(anc_sol.shape, kept),
            dma((2, 2 + ancestors)),
        ],
        compiler_params=pltpu.CompilerParams(vmem_limit_bytes=62 * 1024 * 1024),
        name="place_results",
    )(leaf_sol, mid_sol, anc_sol)
    return (leaf_sol[None, None, None, None], mid_sol[None, None, None], anc_sol)


def fits_fused(mesh, rhs_count):
    layers, rows, cols = (mesh.shape[name] for name in ("layer", "row", "col"))
    pairs = layers == 2 and rows == 4 and cols % 2 == 0
    return pairs and rhs_count % (layers * rows * 128) == 0


def solution(mesh):
    in_specs = (
        P("layer", "row", "col", None, None, None),
        P("layer", "row", "col", None, None, None),
        P("layer", "row", "col", None, None, None),
        P("layer", "row", "col", None),
        P("layer", "row", "col", None),
        P("layer", "row", "col"),
        P("layer", "row", "col", None, None),
        P("layer", "row", "col", None, None),
        P("layer", "row", "col", None, None, None),
        P(),
        P(),
        P(),
    )
    out_specs = (
        P("layer", "row", "col", None, None, None),
        P("layer", "row", "col", None, None),
        P(),
    )

    def run(leaf_rhs, *rest):
        chosen = body
        if fits_fused(mesh, leaf_rhs.shape[-1]) and leaf_rhs.shape[3] == 1:
            sizes = (mesh.shape[name] for name in ("layer", "row", "col"))
            chosen = functools.partial(fused_body, *sizes)
        return jax.shard_map(
            chosen, mesh=mesh, in_specs=in_specs, out_specs=out_specs, check_vma=False
        )(leaf_rhs, *rest)

    return run
```

```python
import functools

import jax
import jax.numpy as jnp
from jax import lax
from jax.experimental import pallas as pl
from jax.experimental.pallas import tpu as pltpu
from jax.sharding import PartitionSpec as P

MESH = pl.DeviceIdType.MESH
LAG_END, LAG_INSIDE = 7, 3


def solve_ancestors(partial_rows, rhs_rows, anc_inv, anc_lower):
    solved = []
    for anc_index in range(anc_inv.shape[0]):
        running = rhs_rows[anc_index].astype(jnp.float32) - partial_rows[anc_index]
        if anc_index > 0:
            offset = anc_index * (anc_index - 1) // 2
            earlier = anc_lower[offset : offset + anc_index]
            running = running - jnp.einsum(
                "bsj,bjt->st", earlier, jnp.stack(solved), preferred_element_type=jnp.float32
            )
        residue = running.astype(jnp.bfloat16)
        solved.append(
            jnp.dot(anc_inv[anc_index], residue, preferred_element_type=jnp.float32).astype(
                jnp.bfloat16
            )
        )
    return jnp.stack(solved)


def add_slots(received):
    return jnp.sum(received, axis=0)


def body(
    leaf_rhs,
    leaf_inv,
    leaf_blocks,
    block_col,
    block_row,
    block_count,
    mid_rhs,
    mid_inv,
    anc_blocks,
    anc_rhs,
    anc_inv,
    anc_lower,
):
    leaf_sol = jnp.einsum(
        "ksj,kjt->kst", leaf_inv[0, 0, 0], leaf_rhs[0, 0, 0], preferred_element_type=jnp.float32
    ).astype(jnp.bfloat16)
    factor_blocks = leaf_blocks[0, 0, 0]
    columns = block_col[0, 0, 0]
    targets = block_row[0, 0, 0]
    live_count = block_count[0, 0, 0]
    grid_cols = lax.axis_size("col")
    empty_term = jnp.zeros((grid_cols,) + leaf_sol.shape[1:], jnp.float32)
    piece = lax.all_gather(leaf_sol, "row", axis=0, tiled=True)
    piece_rows = piece.shape[0]

    def one_block(slot_index, current_sum):
        column = columns[slot_index]
        inside = (column >= 0) & (column < piece_rows)

        def add_one(partial_sum):
            chosen = lax.dynamic_index_in_dim(
                piece, jnp.clip(column, 0, piece_rows - 1), 0, keepdims=False
            )
            product = jnp.dot(factor_blocks[slot_index], chosen, preferred_element_type=jnp.float32)
            row_now = lax.dynamic_index_in_dim(partial_sum, targets[slot_index], 0, keepdims=False)
            return lax.dynamic_update_index_in_dim(
                partial_sum, row_now + product, targets[slot_index], 0
            )

        return lax.cond(inside, add_one, lambda unchanged: unchanged, current_sum)

    mid_terms = lax.fori_loop(0, live_count, one_block, empty_term)
    mid_own = add_slots(lax.all_to_all(mid_terms, "col", split_axis=0, concat_axis=0, tiled=True))
    residue = (mid_rhs[0, 0, 0].astype(jnp.float32) - mid_own).astype(jnp.bfloat16)
    mid_sol = jnp.dot(mid_inv[0, 0, 0], residue, preferred_element_type=jnp.float32).astype(
        jnp.bfloat16
    )
    anc_term = jnp.einsum(
        "asj,jt->ast", anc_blocks[0, 0, 0], mid_sol, preferred_element_type=jnp.float32
    )
    anc_part = lax.psum(anc_term, ("layer", "row", "col"))
    anc_sol = solve_ancestors(anc_part, anc_rhs, anc_inv, anc_lower)
    return (leaf_sol[None, None, None], mid_sol[None, None, None], anc_sol)


def fused_kernel(
    layers,
    rows,
    cols,
    block_col_h,
    block_row_h,
    block_count_h,
    leaf_rhs_h,
    leaf_inv_h,
    blocks_h,
    mid_rhs_h,
    mid_inv_h,
    anc_blocks_h,
    anc_rhs_h,
    anc_inv_h,
    anc_lower_h,
    leaf_out,
    mid_out,
    anc_out,
    block_col,
    block_row,
    block_count,
    leaf_rhs,
    leaf_inv,
    blocks,
    mid_rhs,
    mid_inv,
    anc_rhs,
    anc_inv,
    anc_lower,
    xs,
    dense,
    from_left,
    from_right,
    outgoing,
    acc,
    terms,
    own_terms,
    mid_own,
    mids,
    ancb,
    part_out,
    part_outer,
    part_inner,
    total,
    sol,
    load_sem,
    store_sem,
    a_send,
    a_recv,
    b_send,
    b_recv,
    m_send,
    m_recv,
    g_send,
    g_recv,
    c_send,
    c_recv,
    s_send,
    s_recv,
):
    layer, row, col = (lax.axis_index(name) for name in ("layer", "row", "col"))
    plane = layers * rows
    size, width = mid_own.shape[1:]
    ancestors = sol.shape[0]
    max_blocks = blocks.shape[0]
    half = cols // 2
    sib_row = (row // 2) * 2 + 1 - row % 2
    far_row = (row + rows // 2) % rows
    far_sib_row = (far_row // 2) * 2 + 1 - far_row % 2
    other = (layer + 1) % layers
    sib, across, far = (layer, sib_row, col), (other, row, col), (layer, far_row, col)

    def slot(of_layer, of_row):
        return of_layer * rows + of_row

    me = slot(layer, row)

    def remote(src, dst, send_sem, recv_sem, device):
        return pltpu.make_async_remote_copy(
            src_ref=src,
            dst_ref=dst,
            send_sem=send_sem,
            recv_sem=recv_sem,
            device_id=device,
            device_id_type=MESH,
        )

    def lanes(index):
        return pl.ds(pl.multiple_of(index * width, width), width)

    def depth_of(which):
        return pl.ds(pl.multiple_of(which * size, size), size)

    loads = [
        pltpu.make_async_copy(src, dst, load_sem.at[i])
        for i, (src, dst) in enumerate(
            [
                (leaf_inv_h, leaf_inv),
                (leaf_rhs_h, leaf_rhs),
                (anc_blocks_h, ancb.at[:, :, depth_of(me)]),
                (blocks_h, blocks),
                (mid_rhs_h, mid_rhs),
                (mid_inv_h, mid_inv),
                (anc_rhs_h.at[:, :, lanes(me)], anc_rhs),
                (anc_inv_h, anc_inv),
                (anc_lower_h, anc_lower),
                (block_col_h, block_col),
                (block_row_h, block_row),
                (block_count_h, block_count),
            ]
        )
    ]
    for load in loads:
        load.start()

    barrier = pltpu.get_barrier_semaphore()
    for step in range(1, plane):
        peer = (me + step) % plane
        pl.semaphore_signal(
            barrier, inc=1, device_id=(peer // rows, peer % rows, col), device_id_type=MESH
        )

    @pl.when(col > 0)
    def _():
        pl.semaphore_signal(barrier, inc=1, device_id=(layer, row, col - 1), device_id_type=MESH)

    @pl.when(col < cols - 1)
    def _():
        pl.semaphore_signal(barrier, inc=1, device_id=(layer, row, col + 1), device_id_type=MESH)

    loads[0].wait()
    loads[1].wait()
    ends = (col == 0).astype(jnp.int32) + (col == cols - 1).astype(jnp.int32)
    pl.semaphore_wait(barrier, plane + 1 - ends)

    def leaf_chunk(j, kind):
        at_row = (row, row, far_row)[kind]
        to = (sib, far, sib)[kind]
        ref = xs.at[j, at_row]
        return remote(ref, ref, a_send.at[kind, j], a_recv.at[kind, j], to)

    def leaf_arrival(j, kind):
        at_row = (sib_row, far_row, far_sib_row)[kind]
        ref = xs.at[j, at_row]
        return remote(ref, ref, a_send.at[kind, j], a_recv.at[kind, j], sib)

    def leaf_store(j):
        return pltpu.make_async_copy(
            xs.at[j, row], leaf_out.at[:, lanes(j)], store_sem.at[0, j]
        )

    def leaf_step(j, carry):
        xs[j, row] = jnp.dot(
            leaf_inv[...], leaf_rhs[:, lanes(j)], preferred_element_type=jnp.float32
        ).astype(xs.dtype)
        leaf_chunk(j, 1).start()
        leaf_chunk(j, 0).start()
        leaf_store(j).start()
        return carry

    lax.fori_loop(0, plane, leaf_step, 0)

    first = ancestors // 2

    def block_ref(which, kind):
        part = {5: slice(0, first), 6: slice(first, ancestors)}.get(kind, slice(0, ancestors))
        return ancb.at[part, :, depth_of(which)]

    def block_copy(kind):
        beside, beyond = slot(other, row), slot(layer, far_row)
        which = (me, me, me, beside, beyond, beyond, beside, slot(other, far_row))[kind]
        to = (sib, across, far, sib, sib, across, far, sib)[kind]
        ref = block_ref(which, kind)
        return remote(ref, ref, g_send.at[kind], g_recv.at[kind], to)

    def block_arrival(kind):
        which = (
            slot(layer, sib_row),
            slot(other, row),
            slot(layer, far_row),
            slot(other, sib_row),
            slot(layer, far_sib_row),
            slot(other, far_row),
            slot(other, far_row),
            slot(other, far_sib_row),
        )[kind]
        ref = block_ref(which, kind)
        return remote(ref, ref, g_send.at[kind], g_recv.at[kind], sib)

    loads[2].wait()
    block_copy(1).start()
    block_copy(2).start()
    block_copy(0).start()

    for load in loads[9:] + loads[3:4]:
        load.wait()

    def place_target(m, carry):
        for i in range(rows):
            found = jnp.int32(max_blocks)
            for n in range(max_blocks):
                hit = (block_col[n] == i) & (block_row[n] == m) & (n < block_count[0, 0, 0])
                found = jnp.where(hit, n, found)
            there = found < max_blocks
            block = blocks[jnp.minimum(found, max_blocks - 1)]
            keep = jnp.full(block.shape, there.astype(jnp.int32)) > 0
            dense[m, :, i * size : (i + 1) * size] = jnp.where(
                keep, block.astype(jnp.float32), 0.0
            ).astype(dense.dtype)
        return carry

    lax.fori_loop(0, cols, place_target, 0)

    def gathered(j):
        return xs[j].reshape(rows * size, width)

    def sum_copy(j, m, buffer, to):
        return remote(outgoing.at[j, m], buffer.at[j, m], b_send.at[j, m], b_recv_of(buffer, j, m), to)

    def b_recv_of(buffer, j, m):
        return b_recv.at[0 if buffer is from_left else 1, j, m]

    def sums_on(j, m, buffer, has_more, to):
        outgoing_sum = terms[m]

        @pl.when(has_more)
        def _():
            sum_copy(j, m, buffer, to).wait_recv()
            outgoing[j, m] = (outgoing_sum + buffer[j, m].astype(jnp.float32)).astype(
                outgoing.dtype
            )

        @pl.when(jnp.logical_not(has_more))
        def _():
            outgoing[j, m] = outgoing_sum.astype(outgoing.dtype)

        sum_copy(j, m, buffer, to).start()

    def mid_copy(j):
        return remote(
            mid_own.at[j], mids.at[me], m_send.at[j], m_recv.at[me], (j // rows, j % rows, col)
        )

    def mid_store(j):
        return pltpu.make_async_copy(mid_own.at[j], mid_out.at[:, lanes(j)], store_sem.at[1, j])

    def forward_leaf(j):
        leaf_arrival(j, 1).wait_recv()
        leaf_chunk(j, 2).start()

    loads[4].wait()
    loads[5].wait()
    forward_leaf(0)
    at_end = (col == 0) | (col == cols - 1)
    lag = jnp.where(at_end, LAG_END, LAG_INSIDE)
    relay_at = jnp.where(at_end, 6, 5)

    def sum_step(j, carry):
        @pl.when(j < plane)
        def _():
            @pl.when(j < plane - 1)
            def _():
                forward_leaf(j + 1)

            leaf_arrival(j, 0).wait_recv()
            leaf_arrival(j, 2).wait_recv()
            terms[...] = jnp.dot(
                dense[...].reshape(cols * size, rows * size),
                gathered(j),
                preferred_element_type=jnp.float32,
            ).reshape(cols, size, width)
            own_terms[j] = terms[col]
            for distance in range(cols - 1, 0, -1):

                @pl.when(col + distance < cols)
                def _():
                    sums_on(j, col + distance, from_left, col > 0, (layer, row, col + 1))

                @pl.when(col - distance >= 0)
                def _():
                    sums_on(j, col - distance, from_right, col < cols - 1, (layer, row, col - 1))

        @pl.when(j == 3)
        def _():
            block_arrival(1).wait_recv()
            block_copy(6).start()
            block_copy(3).start()

        @pl.when(j == relay_at)
        def _():
            block_arrival(2).wait_recv()
            block_copy(5).start()
            block_copy(4).start()

        @pl.when(j == plane)
        def _():
            block_arrival(5).wait_recv()
            block_arrival(6).wait_recv()
            block_copy(7).start()

        @pl.when((j >= lag) & (j < plane + lag))
        def _():
            done = j - lag
            acc[...] = mid_rhs[:, lanes(done)].astype(jnp.float32) - own_terms[done]

            @pl.when(col > 0)
            def _():
                sum_copy(done, col, from_left, sib).wait_recv()
                acc[...] -= from_left[done, col].astype(jnp.float32)

            @pl.when(col < cols - 1)
            def _():
                sum_copy(done, col, from_right, sib).wait_recv()
                acc[...] -= from_right[done, col].astype(jnp.float32)

            solved = jnp.dot(
                mid_inv[...], acc[...].astype(jnp.bfloat16), preferred_element_type=jnp.float32
            ).astype(jnp.bfloat16)
            mid_own[done] = solved

            @pl.when(done == me)
            def _():
                mids[me] = solved

            @pl.when(done != me)
            def _():
                mid_copy(done).start()

            mid_store(done).start()

        return carry

    lax.fori_loop(0, plane + max(LAG_END, LAG_INSIDE), sum_step, 0)

    for kind in (0, 3, 4, 7):
        block_arrival(kind).wait_recv()
    for step in range(1, plane):
        peer = (me + step) % plane
        remote(mids.at[peer], mids.at[peer], m_send.at[0], m_recv.at[peer], sib).wait_recv()
    for load in loads[6:9]:
        load.wait()

    in_left = col < half
    inward = (layer, row, jnp.where(in_left, col + 1, col - 1))
    outward = (layer, row, jnp.where(in_left, col - 1, col + 1))
    middle = (col == half - 1) | (col == half)
    has_outer = (col > 0) & (col < cols - 1)

    def up_copy(a, buffer, kind, to):
        return remote(part_out.at[a], buffer.at[a], c_send.at[0, a], c_recv.at[kind, a], to)

    def down_copy(a):
        return remote(total.at[a], part_inner.at[a], c_send.at[1, a], c_recv.at[1, a], outward)

    def sum_up(a):
        acc[...] = jnp.dot(
            ancb[a], mids[...].reshape(plane * size, width), preferred_element_type=jnp.float32
        )

        @pl.when(has_outer)
        def _():
            up_copy(a, part_outer, 0, sib).wait_recv()
            acc[...] += part_outer[a].astype(jnp.float32)

        part_out[a] = acc[...].astype(part_out.dtype)

        @pl.when(middle)
        def _():
            up_copy(a, part_inner, 1, inward).start()

        @pl.when(jnp.logical_not(middle))
        def _():
            up_copy(a, part_outer, 0, inward).start()

    def sol_ref(a, which):
        return anc_out.at[a, :, lanes(which)]

    def sol_copy(a, kind):
        turn = a % 2
        which = (
            me,
            me,
            me,
            slot(other, row),
            slot(layer, far_row),
            (slot(other, row), slot(layer, far_row))[turn],
            slot(other, far_row),
        )[kind]
        to = (sib, across, far, sib, sib, (far, across)[turn], sib)[kind]
        src = sol.at[a] if kind < 3 else sol_ref(a, which)
        return remote(src, sol_ref(a, which), s_send.at[kind, a], s_recv.at[kind, a], to)

    def sol_arrival(a, kind):
        which = (
            slot(layer, sib_row),
            slot(other, row),
            slot(layer, far_row),
            slot(other, sib_row),
            slot(layer, far_sib_row),
            slot(other, far_row),
            slot(other, far_sib_row),
        )[kind]
        return remote(sol.at[a], sol_ref(a, which), s_send.at[kind, a], s_recv.at[kind, a], sib)

    def sol_store(a):
        return pltpu.make_async_copy(sol.at[a], sol_ref(a, me), store_sem.at[2, a])

    def total_down(a, of_middle):
        @pl.when(middle if of_middle else jnp.logical_not(middle))
        def _():
            up_copy(a, part_inner, 1, sib).wait_recv()
            value = part_inner[a].astype(jnp.float32)
            if of_middle:
                value += part_out[a].astype(jnp.float32)
            total[a] = value.astype(total.dtype)

            @pl.when(has_outer)
            def _():
                down_copy(a).start()

    def solve(a):
        running = anc_rhs[a].astype(jnp.float32) - total[a].astype(jnp.float32)
        offset = a * (a - 1) // 2
        for b in range(a):
            running -= jnp.dot(anc_lower[offset + b], sol[b], preferred_element_type=jnp.float32)
        sol[a] = jnp.dot(
            anc_inv[a], running.astype(jnp.bfloat16), preferred_element_type=jnp.float32
        ).astype(sol.dtype)
        for kind in (2, 1, 0):
            sol_copy(a, kind).start()
        sol_store(a).start()

    def relay(a):
        for kind in ((1, 2), (2, 1))[a % 2]:
            sol_arrival(a, kind).wait_recv()
            if kind == 1 + a % 2:
                sol_copy(a, 5).start()
            sol_copy(a, kind + 2).start()
    for a in range(ancestors + 2):
        if a < ancestors:
            sum_up(a)
        if a >= 2:
            total_down(a - 2, True)
    for a in range(ancestors):
        total_down(a, False)
        solve(a)
    for a in range(ancestors):
        relay(a)
    for a in range(ancestors):
        sol_arrival(a, 5).wait_recv()
        sol_copy(a, 6).start()

    def drain(j, carry):
        for kind in range(3):
            leaf_chunk(j, kind).wait_send()
        leaf_store(j).wait()
        mid_store(j).wait()

        @pl.when(j != me)
        def _():
            mid_copy(j).wait_send()

        def drain_sums(m, inner):
            @pl.when(m != col)
            def _():
                sum_copy(j, m, from_left, sib).wait_send()

            return inner

        lax.fori_loop(0, cols, drain_sums, 0)
        return carry

    lax.fori_loop(0, plane, drain, 0)
    for kind in range(8):
        block_copy(kind).wait_send()
    for a in range(ancestors):
        up_copy(a, part_inner, 1, sib).wait_send()

        @pl.when(has_outer)
        def _():
            down_copy(a).wait_send()

        for kind in range(7):
            sol_copy(a, kind).wait_send()
        sol_store(a).wait()
        for kind in (0, 3, 4, 6):
            sol_arrival(a, kind).wait_recv()


def place_results(leaf_in, mid_in, anc_in, leaf_out, mid_out, anc_out, held, anc_held, sem):
    ancestors = anc_in.shape[0]
    parts = [(anc_in.at[a], anc_held.at[a], anc_out.at[a]) for a in range(ancestors)]
    parts.append((leaf_in, held.at[0], leaf_out))
    parts.append((mid_in, held.at[1], mid_out))
    reads = [pltpu.make_async_copy(a, b, sem.at[0, i]) for i, (a, b, _) in enumerate(parts)]
    writes = [pltpu.make_async_copy(b, c, sem.at[1, i]) for i, (_, b, c) in enumerate(parts)]
    for read in reads:
        read.start()
    for read, write in zip(reads, writes):
        read.wait()
        write.start()
    for write in writes:
        write.wait()


def fused_body(
    layers,
    rows,
    cols,
    leaf_rhs,
    leaf_inv,
    leaf_blocks,
    block_col,
    block_row,
    block_count,
    mid_rhs,
    mid_inv,
    anc_blocks,
    anc_rhs,
    anc_inv,
    anc_lower,
):
    plane = layers * rows
    size, rhs_count = mid_rhs.shape[-2:]
    ancestors = anc_inv.shape[0]
    max_blocks = leaf_blocks.shape[3]
    width = rhs_count // plane
    kept = mid_rhs.dtype
    anywhere = pl.BlockSpec(memory_space=pl.ANY)
    hbm = pl.BlockSpec(memory_space=pltpu.HBM)
    dma = pltpu.SemaphoreType.DMA
    vmem = pltpu.VMEM
    leaf_sol, mid_sol, anc_sol = pl.pallas_call(
        functools.partial(fused_kernel, layers, rows, cols),
        out_shape=[
            jax.ShapeDtypeStruct((size, rhs_count), kept),
            jax.ShapeDtypeStruct((size, rhs_count), kept),
            jax.ShapeDtypeStruct((ancestors, size, rhs_count), kept),
        ],
        in_specs=[hbm] * 12,
        out_specs=[anywhere] * 3,
        scratch_shapes=[
            pltpu.SMEM((max_blocks,), jnp.int32),
            pltpu.SMEM((max_blocks,), jnp.int32),
            pltpu.SMEM(block_count.shape, jnp.int32),
            vmem((size, rhs_count), kept),
            vmem((size, size), kept),
            vmem((max_blocks, size, size), kept),
            vmem((size, rhs_count), kept),
            vmem((size, size), kept),
            vmem((ancestors, size, width), kept),
            vmem(anc_inv.shape, kept),
            vmem(anc_lower.shape, kept),
            vmem((plane, rows, size, width), kept),
            vmem((cols, size, rows * size), kept),
            vmem((plane, cols, size, width), kept),
            vmem((plane, cols, size, width), kept),
            vmem((plane, cols, size, width), kept),
            vmem((size, width), jnp.float32),
            vmem((cols, size, width), jnp.float32),
            vmem((plane, size, width), jnp.float32),
            vmem((plane, size, width), kept),
            vmem((plane, size, width), kept),
            vmem((ancestors, size, plane * size), kept),
            vmem((ancestors, size, width), kept),
            vmem((ancestors, size, width), kept),
            vmem((ancestors, size, width), kept),
            vmem((ancestors, size, width), kept),
            vmem((ancestors, size, width), kept),
            dma((12,)),
            dma((3, max(plane, ancestors))),
            dma((3, plane)),
            dma((3, plane)),
            dma((plane, cols)),
            dma((2, plane, cols)),
            dma((plane,)),
            dma((plane,)),
            dma((8,)),
            dma((8,)),
            dma((2, ancestors)),
            dma((2, ancestors)),
            dma((7, ancestors)),
            dma((7, ancestors)),
        ],
        compiler_params=pltpu.CompilerParams(
            collective_id=0, has_side_effects=True, vmem_limit_bytes=62 * 1024 * 1024
        ),
        name="fused_solve",
    )(
        block_col[0, 0, 0],
        block_row[0, 0, 0],
        block_count,
        leaf_rhs[0, 0, 0, 0],
        leaf_inv[0, 0, 0, 0],
        leaf_blocks[0, 0, 0],
        mid_rhs[0, 0, 0],
        mid_inv[0, 0, 0],
        anc_blocks[0, 0, 0],
        anc_rhs,
        anc_inv,
        anc_lower,
    )
    leaf_sol, mid_sol, anc_sol = pl.pallas_call(
        place_results,
        out_shape=[
            jax.ShapeDtypeStruct(value.shape, kept) for value in (leaf_sol, mid_sol, anc_sol)
        ],
        in_specs=[hbm] * 3,
        out_specs=[hbm] * 3,
        scratch_shapes=[
            vmem((2, size, rhs_count), kept),
            vmem(anc_sol.shape, kept),
            dma((2, 2 + ancestors)),
        ],
        compiler_params=pltpu.CompilerParams(vmem_limit_bytes=62 * 1024 * 1024),
        name="place_results",
    )(leaf_sol, mid_sol, anc_sol)
    return (leaf_sol[None, None, None, None], mid_sol[None, None, None], anc_sol)


def fits_fused(mesh, rhs_count, ancestors):
    layers, rows, cols = (mesh.shape[name] for name in ("layer", "row", "col"))
    pairs = layers == 2 and rows == 4 and cols % 2 == 0 and ancestors > 1
    return pairs and rhs_count % (layers * rows * 128) == 0


def solution(mesh):
    in_specs = (
        P("layer", "row", "col", None, None, None),
        P("layer", "row", "col", None, None, None),
        P("layer", "row", "col", None, None, None),
        P("layer", "row", "col", None),
        P("layer", "row", "col", None),
        P("layer", "row", "col"),
        P("layer", "row", "col", None, None),
        P("layer", "row", "col", None, None),
        P("layer", "row", "col", None, None, None),
        P(),
        P(),
        P(),
    )
    out_specs = (
        P("layer", "row", "col", None, None, None),
        P("layer", "row", "col", None, None),
        P(),
    )

    def run(leaf_rhs, *rest):
        chosen = body
        if fits_fused(mesh, leaf_rhs.shape[-1], rest[-2].shape[0]) and leaf_rhs.shape[3] == 1:
            sizes = (mesh.shape[name] for name in ("layer", "row", "col"))
            chosen = functools.partial(fused_body, *sizes)
        return jax.shard_map(
            chosen, mesh=mesh, in_specs=in_specs, out_specs=out_specs, check_vma=False
        )(leaf_rhs, *rest)

    return run
```

```python
import functools

import jax
import jax.numpy as jnp
from jax import lax
from jax.experimental import pallas as pl
from jax.experimental.pallas import tpu as pltpu
from jax.sharding import PartitionSpec as P

MESH = pl.DeviceIdType.MESH
LAG_END, LAG_INSIDE = 7, 3


def solve_ancestors(partial_rows, rhs_rows, anc_inv, anc_lower):
    solved = []
    for anc_index in range(anc_inv.shape[0]):
        running = rhs_rows[anc_index].astype(jnp.float32) - partial_rows[anc_index]
        if anc_index > 0:
            offset = anc_index * (anc_index - 1) // 2
            earlier = anc_lower[offset : offset + anc_index]
            running = running - jnp.einsum(
                "bsj,bjt->st", earlier, jnp.stack(solved), preferred_element_type=jnp.float32
            )
        residue = running.astype(jnp.bfloat16)
        solved.append(
            jnp.dot(anc_inv[anc_index], residue, preferred_element_type=jnp.float32).astype(
                jnp.bfloat16
            )
        )
    return jnp.stack(solved)


def add_slots(received):
    return jnp.sum(received, axis=0)


def body(
    leaf_rhs,
    leaf_inv,
    leaf_blocks,
    block_col,
    block_row,
    block_count,
    mid_rhs,
    mid_inv,
    anc_blocks,
    anc_rhs,
    anc_inv,
    anc_lower,
):
    leaf_sol = jnp.einsum(
        "ksj,kjt->kst", leaf_inv[0, 0, 0], leaf_rhs[0, 0, 0], preferred_element_type=jnp.float32
    ).astype(jnp.bfloat16)
    factor_blocks = leaf_blocks[0, 0, 0]
    columns = block_col[0, 0, 0]
    targets = block_row[0, 0, 0]
    live_count = block_count[0, 0, 0]
    grid_cols = lax.axis_size("col")
    empty_term = jnp.zeros((grid_cols,) + leaf_sol.shape[1:], jnp.float32)
    piece = lax.all_gather(leaf_sol, "row", axis=0, tiled=True)
    piece_rows = piece.shape[0]

    def one_block(slot_index, current_sum):
        column = columns[slot_index]
        inside = (column >= 0) & (column < piece_rows)

        def add_one(partial_sum):
            chosen = lax.dynamic_index_in_dim(
                piece, jnp.clip(column, 0, piece_rows - 1), 0, keepdims=False
            )
            product = jnp.dot(factor_blocks[slot_index], chosen, preferred_element_type=jnp.float32)
            row_now = lax.dynamic_index_in_dim(partial_sum, targets[slot_index], 0, keepdims=False)
            return lax.dynamic_update_index_in_dim(
                partial_sum, row_now + product, targets[slot_index], 0
            )

        return lax.cond(inside, add_one, lambda unchanged: unchanged, current_sum)

    mid_terms = lax.fori_loop(0, live_count, one_block, empty_term)
    mid_own = add_slots(lax.all_to_all(mid_terms, "col", split_axis=0, concat_axis=0, tiled=True))
    residue = (mid_rhs[0, 0, 0].astype(jnp.float32) - mid_own).astype(jnp.bfloat16)
    mid_sol = jnp.dot(mid_inv[0, 0, 0], residue, preferred_element_type=jnp.float32).astype(
        jnp.bfloat16
    )
    anc_term = jnp.einsum(
        "asj,jt->ast", anc_blocks[0, 0, 0], mid_sol, preferred_element_type=jnp.float32
    )
    anc_part = lax.psum(anc_term, ("layer", "row", "col"))
    anc_sol = solve_ancestors(anc_part, anc_rhs, anc_inv, anc_lower)
    return (leaf_sol[None, None, None], mid_sol[None, None, None], anc_sol)


def fused_kernel(
    layers,
    rows,
    cols,
    block_col_h,
    block_row_h,
    block_count_h,
    leaf_rhs_h,
    leaf_inv_h,
    blocks_h,
    mid_rhs_h,
    mid_inv_h,
    anc_blocks_h,
    anc_rhs_h,
    anc_inv_h,
    anc_lower_h,
    leaf_out,
    mid_out,
    anc_out,
    block_col,
    block_row,
    block_count,
    leaf_rhs,
    leaf_inv,
    blocks,
    mid_rhs,
    mid_inv,
    anc_rhs,
    anc_inv,
    anc_lower,
    xs,
    dense,
    from_left,
    from_right,
    outgoing,
    acc,
    terms,
    own_terms,
    mid_own,
    mids,
    ancb,
    part_out,
    part_outer,
    part_inner,
    total,
    sol,
    load_sem,
    store_sem,
    a_send,
    a_recv,
    b_send,
    b_recv,
    m_send,
    m_recv,
    g_send,
    g_recv,
    c_send,
    c_recv,
    s_send,
    s_recv,
):
    layer, row, col = (lax.axis_index(name) for name in ("layer", "row", "col"))
    plane = layers * rows
    size, width = mid_own.shape[1:]
    ancestors = sol.shape[0]
    max_blocks = blocks.shape[0]
    half = cols // 2
    sib_row = (row // 2) * 2 + 1 - row % 2
    far_row = (row + rows // 2) % rows
    far_sib_row = (far_row // 2) * 2 + 1 - far_row % 2
    other = (layer + 1) % layers
    sib, across, far = (layer, sib_row, col), (other, row, col), (layer, far_row, col)

    def slot(of_layer, of_row):
        return of_layer * rows + of_row

    me = slot(layer, row)

    def remote(src, dst, send_sem, recv_sem, device):
        return pltpu.make_async_remote_copy(
            src_ref=src,
            dst_ref=dst,
            send_sem=send_sem,
            recv_sem=recv_sem,
            device_id=device,
            device_id_type=MESH,
        )

    def lanes(index):
        return pl.ds(pl.multiple_of(index * width, width), width)

    def depth_of(which):
        return pl.ds(pl.multiple_of(which * size, size), size)

    loads = [
        pltpu.make_async_copy(src, dst, load_sem.at[i])
        for i, (src, dst) in enumerate(
            [
                (leaf_inv_h, leaf_inv),
                (leaf_rhs_h, leaf_rhs),
                (anc_blocks_h, ancb.at[:, :, depth_of(me)]),
                (blocks_h, blocks),
                (mid_rhs_h, mid_rhs),
                (mid_inv_h, mid_inv),
                (anc_rhs_h.at[:, :, lanes(me)], anc_rhs),
                (anc_inv_h, anc_inv),
                (anc_lower_h, anc_lower),
                (block_col_h, block_col),
                (block_row_h, block_row),
                (block_count_h, block_count),
            ]
        )
    ]
    for load in loads:
        load.start()

    barrier = pltpu.get_barrier_semaphore()
    for step in range(1, plane):
        peer = (me + step) % plane
        pl.semaphore_signal(
            barrier, inc=1, device_id=(peer // rows, peer % rows, col), device_id_type=MESH
        )

    @pl.when(col > 0)
    def _():
        pl.semaphore_signal(barrier, inc=1, device_id=(layer, row, col - 1), device_id_type=MESH)

    @pl.when(col < cols - 1)
    def _():
        pl.semaphore_signal(barrier, inc=1, device_id=(layer, row, col + 1), device_id_type=MESH)

    loads[0].wait()
    loads[1].wait()
    ends = (col == 0).astype(jnp.int32) + (col == cols - 1).astype(jnp.int32)
    pl.semaphore_wait(barrier, plane + 1 - ends)

    def leaf_chunk(j, kind):
        at_row = (row, row, far_row)[kind]
        to = (sib, far, sib)[kind]
        ref = xs.at[j, at_row]
        return remote(ref, ref, a_send.at[kind, j], a_recv.at[kind, j], to)

    def leaf_arrival(j, kind):
        at_row = (sib_row, far_row, far_sib_row)[kind]
        ref = xs.at[j, at_row]
        return remote(ref, ref, a_send.at[kind, j], a_recv.at[kind, j], sib)

    def leaf_store(j):
        return pltpu.make_async_copy(
            xs.at[j, row], leaf_out.at[:, lanes(j)], store_sem.at[0, j]
        )

    def leaf_step(j, carry):
        xs[j, row] = jnp.dot(
            leaf_inv[...], leaf_rhs[:, lanes(j)], preferred_element_type=jnp.float32
        ).astype(xs.dtype)
        leaf_chunk(j, 1).start()
        leaf_chunk(j, 0).start()
        leaf_store(j).start()
        return carry

    lax.fori_loop(0, plane, leaf_step, 0)

    first = ancestors // 2

    def block_ref(which, kind):
        part = {5: slice(0, first), 6: slice(first, ancestors)}.get(kind, slice(0, ancestors))
        return ancb.at[part, :, depth_of(which)]

    def block_copy(kind):
        beside, beyond = slot(other, row), slot(layer, far_row)
        which = (me, me, me, beside, beyond, beyond, beside, slot(other, far_row))[kind]
        to = (sib, across, far, sib, sib, across, far, sib)[kind]
        ref = block_ref(which, kind)
        return remote(ref, ref, g_send.at[kind], g_recv.at[kind], to)

    def block_arrival(kind):
        which = (
            slot(layer, sib_row),
            slot(other, row),
            slot(layer, far_row),
            slot(other, sib_row),
            slot(layer, far_sib_row),
            slot(other, far_row),
            slot(other, far_row),
            slot(other, far_sib_row),
        )[kind]
        ref = block_ref(which, kind)
        return remote(ref, ref, g_send.at[kind], g_recv.at[kind], sib)

    loads[2].wait()
    block_copy(1).start()
    block_copy(2).start()
    block_copy(0).start()

    for load in loads[9:] + loads[3:4]:
        load.wait()

    def place_target(m, carry):
        for i in range(rows):
            found = jnp.int32(max_blocks)
            for n in range(max_blocks):
                hit = (block_col[n] == i) & (block_row[n] == m) & (n < block_count[0, 0, 0])
                found = jnp.where(hit, n, found)
            there = found < max_blocks
            block = blocks[jnp.minimum(found, max_blocks - 1)]
            keep = jnp.full(block.shape, there.astype(jnp.int32)) > 0
            dense[m, :, i * size : (i + 1) * size] = jnp.where(
                keep, block.astype(jnp.float32), 0.0
            ).astype(dense.dtype)
        return carry

    lax.fori_loop(0, cols, place_target, 0)

    def gathered(j):
        return xs[j].reshape(rows * size, width)

    def sum_copy(j, m, buffer, to):
        return remote(outgoing.at[j, m], buffer.at[j, m], b_send.at[j, m], b_recv_of(buffer, j, m), to)

    def b_recv_of(buffer, j, m):
        return b_recv.at[0 if buffer is from_left else 1, j, m]

    def sums_on(j, m, buffer, has_more, to):
        outgoing_sum = terms[m]

        @pl.when(has_more)
        def _():
            sum_copy(j, m, buffer, to).wait_recv()
            outgoing[j, m] = (outgoing_sum + buffer[j, m].astype(jnp.float32)).astype(
                outgoing.dtype
            )

        @pl.when(jnp.logical_not(has_more))
        def _():
            outgoing[j, m] = outgoing_sum.astype(outgoing.dtype)

        sum_copy(j, m, buffer, to).start()

    def mid_copy(j):
        return remote(
            mid_own.at[j], mids.at[me], m_send.at[j], m_recv.at[me], (j // rows, j % rows, col)
        )

    def mid_store(j):
        return pltpu.make_async_copy(mid_own.at[j], mid_out.at[:, lanes(j)], store_sem.at[1, j])

    def forward_leaf(j):
        leaf_arrival(j, 1).wait_recv()
        leaf_chunk(j, 2).start()

    loads[4].wait()
    loads[5].wait()
    forward_leaf(0)
    at_end = (col == 0) | (col == cols - 1)
    lag = jnp.where(at_end, LAG_END, LAG_INSIDE)
    relay_at = jnp.where(at_end, 6, 5)

    def sum_step(j, carry):
        @pl.when(j < plane)
        def _():
            @pl.when(j < plane - 1)
            def _():
                forward_leaf(j + 1)

            leaf_arrival(j, 0).wait_recv()
            leaf_arrival(j, 2).wait_recv()
            terms[...] = jnp.dot(
                dense[...].reshape(cols * size, rows * size),
                gathered(j),
                preferred_element_type=jnp.float32,
            ).reshape(cols, size, width)
            own_terms[j] = terms[col]
            for distance in range(cols - 1, 0, -1):

                @pl.when(col + distance < cols)
                def _():
                    sums_on(j, col + distance, from_left, col > 0, (layer, row, col + 1))

                @pl.when(col - distance >= 0)
                def _():
                    sums_on(j, col - distance, from_right, col < cols - 1, (layer, row, col - 1))

        @pl.when(j == 3)
        def _():
            block_arrival(1).wait_recv()
            block_copy(6).start()
            block_copy(3).start()

        @pl.when(j == relay_at)
        def _():
            block_arrival(2).wait_recv()
            block_copy(5).start()
            block_copy(4).start()

        @pl.when(j == plane)
        def _():
            block_arrival(5).wait_recv()
            block_arrival(6).wait_recv()
            block_copy(7).start()

        @pl.when((j >= lag) & (j < plane + lag))
        def _():
            done = j - lag
            acc[...] = mid_rhs[:, lanes(done)].astype(jnp.float32) - own_terms[done]

            @pl.when(col > 0)
            def _():
                sum_copy(done, col, from_left, sib).wait_recv()
                acc[...] -= from_left[done, col].astype(jnp.float32)

            @pl.when(col < cols - 1)
            def _():
                sum_copy(done, col, from_right, sib).wait_recv()
                acc[...] -= from_right[done, col].astype(jnp.float32)

            solved = jnp.dot(
                mid_inv[...], acc[...].astype(jnp.bfloat16), preferred_element_type=jnp.float32
            ).astype(jnp.bfloat16)
            mid_own[done] = solved

            @pl.when(done == me)
            def _():
                mids[me] = solved

            @pl.when(done != me)
            def _():
                mid_copy(done).start()

            mid_store(done).start()

        return carry

    lax.fori_loop(0, plane + max(LAG_END, LAG_INSIDE), sum_step, 0)

    for kind in (0, 3, 4, 7):
        block_arrival(kind).wait_recv()
    for step in range(1, plane):
        peer = (me + step) % plane
        remote(mids.at[peer], mids.at[peer], m_send.at[0], m_recv.at[peer], sib).wait_recv()
    for load in loads[6:9]:
        load.wait()

    in_left = col < half
    inward = (layer, row, jnp.where(in_left, col + 1, col - 1))
    outward = (layer, row, jnp.where(in_left, col - 1, col + 1))
    middle = (col == half - 1) | (col == half)
    has_outer = (col > 0) & (col < cols - 1)

    def up_copy(a, buffer, kind, to):
        return remote(part_out.at[a], buffer.at[a], c_send.at[0, a], c_recv.at[kind, a], to)

    def down_copy(a):
        return remote(total.at[a], part_inner.at[a], c_send.at[1, a], c_recv.at[1, a], outward)

    def sum_up(a):
        acc[...] = jnp.dot(
            ancb[a], mids[...].reshape(plane * size, width), preferred_element_type=jnp.float32
        )

        @pl.when(has_outer)
        def _():
            up_copy(a, part_outer, 0, sib).wait_recv()
            acc[...] += part_outer[a].astype(jnp.float32)

        part_out[a] = acc[...].astype(part_out.dtype)

        @pl.when(middle)
        def _():
            up_copy(a, part_inner, 1, inward).start()

        @pl.when(jnp.logical_not(middle))
        def _():
            up_copy(a, part_outer, 0, inward).start()

    def sol_ref(a, which):
        return anc_out.at[a, :, lanes(which)]

    def sol_copy(a, kind):
        turn = a % 2
        which = (
            me,
            me,
            me,
            slot(other, row),
            slot(layer, far_row),
            (slot(other, row), slot(layer, far_row))[turn],
            slot(other, far_row),
        )[kind]
        to = (sib, across, far, sib, sib, (far, across)[turn], sib)[kind]
        src = sol.at[a] if kind < 3 else sol_ref(a, which)
        return remote(src, sol_ref(a, which), s_send.at[kind, a], s_recv.at[kind, a], to)

    def sol_arrival(a, kind):
        which = (
            slot(layer, sib_row),
            slot(other, row),
            slot(layer, far_row),
            slot(other, sib_row),
            slot(layer, far_sib_row),
            slot(other, far_row),
            slot(other, far_sib_row),
        )[kind]
        return remote(sol.at[a], sol_ref(a, which), s_send.at[kind, a], s_recv.at[kind, a], sib)

    def sol_store(a):
        return pltpu.make_async_copy(sol.at[a], sol_ref(a, me), store_sem.at[2, a])

    def total_down(a, of_middle):
        @pl.when(middle if of_middle else jnp.logical_not(middle))
        def _():
            up_copy(a, part_inner, 1, sib).wait_recv()
            value = part_inner[a].astype(jnp.float32)
            if of_middle:
                value += part_out[a].astype(jnp.float32)
            total[a] = value.astype(total.dtype)

            @pl.when(has_outer)
            def _():
                down_copy(a).start()

    def solve(a):
        running = anc_rhs[a].astype(jnp.float32) - total[a].astype(jnp.float32)
        offset = a * (a - 1) // 2
        for b in range(a):
            running -= jnp.dot(anc_lower[offset + b], sol[b], preferred_element_type=jnp.float32)
        sol[a] = jnp.dot(
            anc_inv[a], running.astype(jnp.bfloat16), preferred_element_type=jnp.float32
        ).astype(sol.dtype)
        for kind in (2, 1, 0):
            sol_copy(a, kind).start()
        sol_store(a).start()

    def relay(a):
        for kind in ((1, 2), (2, 1))[a % 2]:
            sol_arrival(a, kind).wait_recv()
            if kind == 1 + a % 2:
                sol_copy(a, 5).start()
            sol_copy(a, kind + 2).start()
    for a in range(ancestors + 2):
        if a < ancestors:
            sum_up(a)
        if a >= 2:
            total_down(a - 2, True)
    for a in range(ancestors + 2):
        if a < ancestors:
            total_down(a, False)
            solve(a)
        if a >= 2:
            relay(a - 2)
    for a in range(ancestors):
        sol_arrival(a, 5).wait_recv()
        sol_copy(a, 6).start()

    def drain(j, carry):
        for kind in range(3):
            leaf_chunk(j, kind).wait_send()
        leaf_store(j).wait()
        mid_store(j).wait()

        @pl.when(j != me)
        def _():
            mid_copy(j).wait_send()

        def drain_sums(m, inner):
            @pl.when(m != col)
            def _():
                sum_copy(j, m, from_left, sib).wait_send()

            return inner

        lax.fori_loop(0, cols, drain_sums, 0)
        return carry

    lax.fori_loop(0, plane, drain, 0)
    for kind in range(8):
        block_copy(kind).wait_send()
    for a in range(ancestors):
        up_copy(a, part_inner, 1, sib).wait_send()

        @pl.when(has_outer)
        def _():
            down_copy(a).wait_send()

        for kind in range(7):
            sol_copy(a, kind).wait_send()
        sol_store(a).wait()
        for kind in (0, 3, 4, 6):
            sol_arrival(a, kind).wait_recv()


def place_results(leaf_in, mid_in, anc_in, leaf_out, mid_out, anc_out, held, anc_held, sem):
    ancestors = anc_in.shape[0]
    parts = [(anc_in.at[a], anc_held.at[a], anc_out.at[a]) for a in range(ancestors)]
    parts.append((leaf_in, held.at[0], leaf_out))
    parts.append((mid_in, held.at[1], mid_out))
    reads = [pltpu.make_async_copy(a, b, sem.at[0, i]) for i, (a, b, _) in enumerate(parts)]
    writes = [pltpu.make_async_copy(b, c, sem.at[1, i]) for i, (_, b, c) in enumerate(parts)]
    for read in reads:
        read.start()
    for read, write in zip(reads, writes):
        read.wait()
        write.start()
    for write in writes:
        write.wait()


def fused_body(
    layers,
    rows,
    cols,
    leaf_rhs,
    leaf_inv,
    leaf_blocks,
    block_col,
    block_row,
    block_count,
    mid_rhs,
    mid_inv,
    anc_blocks,
    anc_rhs,
    anc_inv,
    anc_lower,
):
    plane = layers * rows
    size, rhs_count = mid_rhs.shape[-2:]
    ancestors = anc_inv.shape[0]
    max_blocks = leaf_blocks.shape[3]
    width = rhs_count // plane
    kept = mid_rhs.dtype
    anywhere = pl.BlockSpec(memory_space=pl.ANY)
    hbm = pl.BlockSpec(memory_space=pltpu.HBM)
    dma = pltpu.SemaphoreType.DMA
    vmem = pltpu.VMEM
    leaf_sol, mid_sol, anc_sol = pl.pallas_call(
        functools.partial(fused_kernel, layers, rows, cols),
        out_shape=[
            jax.ShapeDtypeStruct((size, rhs_count), kept),
            jax.ShapeDtypeStruct((size, rhs_count), kept),
            jax.ShapeDtypeStruct((ancestors, size, rhs_count), kept),
        ],
        in_specs=[hbm] * 12,
        out_specs=[anywhere] * 3,
        scratch_shapes=[
            pltpu.SMEM((max_blocks,), jnp.int32),
            pltpu.SMEM((max_blocks,), jnp.int32),
            pltpu.SMEM(block_count.shape, jnp.int32),
            vmem((size, rhs_count), kept),
            vmem((size, size), kept),
            vmem((max_blocks, size, size), kept),
            vmem((size, rhs_count), kept),
            vmem((size, size), kept),
            vmem((ancestors, size, width), kept),
            vmem(anc_inv.shape, kept),
            vmem(anc_lower.shape, kept),
            vmem((plane, rows, size, width), kept),
            vmem((cols, size, rows * size), kept),
            vmem((plane, cols, size, width), kept),
            vmem((plane, cols, size, width), kept),
            vmem((plane, cols, size, width), kept),
            vmem((size, width), jnp.float32),
            vmem((cols, size, width), jnp.float32),
            vmem((plane, size, width), jnp.float32),
            vmem((plane, size, width), kept),
            vmem((plane, size, width), kept),
            vmem((ancestors, size, plane * size), kept),
            vmem((ancestors, size, width), kept),
            vmem((ancestors, size, width), kept),
            vmem((ancestors, size, width), kept),
            vmem((ancestors, size, width), kept),
            vmem((ancestors, size, width), kept),
            dma((12,)),
            dma((3, max(plane, ancestors))),
            dma((3, plane)),
            dma((3, plane)),
            dma((plane, cols)),
            dma((2, plane, cols)),
            dma((plane,)),
            dma((plane,)),
            dma((8,)),
            dma((8,)),
            dma((2, ancestors)),
            dma((2, ancestors)),
            dma((7, ancestors)),
            dma((7, ancestors)),
        ],
        compiler_params=pltpu.CompilerParams(
            collective_id=0, has_side_effects=True, vmem_limit_bytes=62 * 1024 * 1024
        ),
        name="fused_solve",
    )(
        block_col[0, 0, 0],
        block_row[0, 0, 0],
        block_count,
        leaf_rhs[0, 0, 0, 0],
        leaf_inv[0, 0, 0, 0],
        leaf_blocks[0, 0, 0],
        mid_rhs[0, 0, 0],
        mid_inv[0, 0, 0],
        anc_blocks[0, 0, 0],
        anc_rhs,
        anc_inv,
        anc_lower,
    )
    leaf_sol, mid_sol, anc_sol = pl.pallas_call(
        place_results,
        out_shape=[
            jax.ShapeDtypeStruct(value.shape, kept) for value in (leaf_sol, mid_sol, anc_sol)
        ],
        in_specs=[hbm] * 3,
        out_specs=[hbm] * 3,
        scratch_shapes=[
            vmem((2, size, rhs_count), kept),
            vmem(anc_sol.shape, kept),
            dma((2, 2 + ancestors)),
        ],
        compiler_params=pltpu.CompilerParams(vmem_limit_bytes=62 * 1024 * 1024),
        name="place_results",
    )(leaf_sol, mid_sol, anc_sol)
    return (leaf_sol[None, None, None, None], mid_sol[None, None, None], anc_sol)


def fits_fused(mesh, rhs_count, ancestors):
    layers, rows, cols = (mesh.shape[name] for name in ("layer", "row", "col"))
    pairs = layers == 2 and rows == 4 and cols % 2 == 0 and ancestors > 1
    return pairs and rhs_count % (layers * rows * 128) == 0


def solution(mesh):
    in_specs = (
        P("layer", "row", "col", None, None, None),
        P("layer", "row", "col", None, None, None),
        P("layer", "row", "col", None, None, None),
        P("layer", "row", "col", None),
        P("layer", "row", "col", None),
        P("layer", "row", "col"),
        P("layer", "row", "col", None, None),
        P("layer", "row", "col", None, None),
        P("layer", "row", "col", None, None, None),
        P(),
        P(),
        P(),
    )
    out_specs = (
        P("layer", "row", "col", None, None, None),
        P("layer", "row", "col", None, None),
        P(),
    )

    def run(leaf_rhs, *rest):
        chosen = body
        if fits_fused(mesh, leaf_rhs.shape[-1], rest[-2].shape[0]) and leaf_rhs.shape[3] == 1:
            sizes = (mesh.shape[name] for name in ("layer", "row", "col"))
            chosen = functools.partial(fused_body, *sizes)
        return jax.shard_map(
            chosen, mesh=mesh, in_specs=in_specs, out_specs=out_specs, check_vma=False
        )(leaf_rhs, *rest)

    return run
```
